256 devices in a mesh: kv: 32 (over y, z), tp: 8 (over x, core).
Axes of the slice: x: 4, y: 4, z: 8, core: 2. Of those that a mesh axis runs over, the one named last changes fastest.
Arguments:
- queries: bfloat16 [1024, 16, 8192], P('kv', None, 'tp'), may hold values from -32 to 32
- suffix_kv: bfloat16 [1024, 16, 8, 256], P('kv', None, 'tp'), may hold values from -12 to 12
- suffix_len: int32 [1024], P('kv'), may hold values from 1 to 16, 10240 in all
- sys_kv: bfloat16 [1024, 8, 256], P('kv', 'tp'), may hold values from -4 to 4
- doc_kv: bfloat16 [32, 1024, 8, 256], P('kv', None, 'tp'), may hold values from -4 to 4
- doc_home: int32 [32], replicated, may hold values from 0 to 31, each once
- doc_of: int32 [1024], P('kv'), may hold values from 0 to 31, as said below
- conv_kv: bfloat16 [512, 256, 8, 256], P('kv', None, 'tp'), may hold values from -4 to 4
- conv_of: int32 [1024], P('kv'), may hold values from 0 to 511, as said below
Outputs:
- attended: bfloat16 [1024, 16, 8192], P(('kv', 'tp'))
The draws below stay inside these ranges and needn't reach their ends.
Inputs may be any that keep to these rules, and one draw needn't show every extreme that they name: `doc_of`: requests of one conversation name the same document. Among the 32 requests of one index of kv, no document is named more than 2 times, and in every draw some document is named exactly 2 times by the requests of every index of kv. `conv_of`: each request's conversation is one of the 16 conversations stored on its own index of kv (conversation c on index c // 16); every conversation is named by exactly two requests.
All inputs are finite; a program needn't handle non-finite values. No bound on the sum of `suffix_len` on one device may be relied on, other than what follows from the above.
Results may differ from the reference program's by a relative error of at most 0.0065.
Values may be sent and summed in bfloat16 or wider, within the bound.
A program may use at most 128 MiB of HBM per device.

```python
import math
from functools import reduce
import jax
import jax.numpy as jnp
import numpy as np
from jax import lax

QUERY_HEADS = 64
KEY_VALUE_HEADS = 8
HEAD_SIZE = 128
REQ_DEV = 32
SUFFIX_TOKENS = 16
DOC_LEN = 1024
CONV_LEN = 256
CONV_DEV = 16
HALF_CAP = 1
REQS = 1024
DOCS = 32
CONVS = 512
SYS_LEN = 1024


def request_tree(key):
    key = jax.random.fold_in(key, 9001)
    key_order, key_score, key_shuffle, key_pair = jax.random.split(key, 4)
    order = jax.random.permutation(key_order, DOCS)
    sequence_entries = DOCS * HALF_CAP
    sequence_place = jnp.arange(sequence_entries, dtype=jnp.int32) // HALF_CAP
    gaussian_jitter = jax.random.randint(key_score, (DOCS, sequence_entries), 0, 1000)
    extra_logit_offset = jnp.where(sequence_place == 0, 100000, jnp.where(sequence_place < 4, 600, 0))
    affinity_logit = (gaussian_jitter + extra_logit_offset[None, :]) * sequence_entries + jnp.arange(sequence_entries, dtype=jnp.int32)[None, :]
    picked = lax.top_k(affinity_logit, CONV_DEV)[1]
    chosen = order[picked // HALF_CAP]
    chosen = jax.random.permutation(key_shuffle, chosen, axis=1, independent=True)
    base_rows = jnp.broadcast_to(jnp.arange(REQ_DEV, dtype=jnp.int32), (DOCS, REQ_DEV))
    pairing = jax.random.permutation(key_pair, base_rows, axis=1, independent=True) // 2
    talks = jnp.arange(DOCS, dtype=jnp.int32)[:, None] * CONV_DEV + pairing
    documents = jnp.take_along_axis(chosen, pairing, axis=1)
    return (documents.reshape(REQS).astype(jnp.int32), talks.reshape(REQS).astype(jnp.int32))


def normal_cache(key, leading_dims, prefix_length, spread):
    key_part, value_part = jax.random.split(key)
    array_shape = leading_dims + (prefix_length, KEY_VALUE_HEADS, HEAD_SIZE)
    keys = jnp.clip(jax.random.normal(key_part, array_shape, jnp.float32) * spread, -4.0 * spread, 4.0 * spread)
    values = jnp.clip(jax.random.normal(value_part, array_shape, jnp.float32), -4.0, 4.0)
    return jnp.concatenate([keys, values], axis=-1).astype(jnp.bfloat16)


def draw_queries(key, part):
    key = jax.random.fold_in(key, 11)
    key_base = jax.random.fold_in(key, 0)
    array_shape = (REQS, SUFFIX_TOKENS, QUERY_HEADS * HEAD_SIZE)
    return jnp.clip(jax.random.normal(key_base, array_shape, jnp.float32), -4.0, 4.0).astype(jnp.bfloat16)


def draw_suffix_kv(key, part):
    key = jax.random.fold_in(key, 21)
    return normal_cache(key, (REQS,), SUFFIX_TOKENS, 3.0)


def draw_sys_kv(key, part):
    key = jax.random.fold_in(key, 31)
    return normal_cache(key, (), SYS_LEN, 1.0)


def draw_doc_kv(key, part):
    key = jax.random.fold_in(key, 41)
    return normal_cache(key, (DOCS,), DOC_LEN, 1.0)


def draw_conv_kv(key, part):
    key = jax.random.fold_in(key, 51)
    return normal_cache(key, (CONVS,), CONV_LEN, 1.0)


def draw_doc_of(key, part):
    documents, talks = request_tree(key)
    return documents


def draw_conv_of(key, part):
    documents, talks = request_tree(key)
    return talks


def profile(count, total, limit, lean):
    portions = [(1 << 20) // math.isqrt(rank ** lean) + 1 for rank in range(2, count + 1)]
    spare, holding = total - limit - (count - 1), [1] * (count - 1)
    while spare > 0:
        movable = [i for i in range(count - 1) if holding[i] < limit]
        mass, left = sum([portions[i] for i in movable]), spare
        for i in movable:
            more = min(limit - holding[i], max(1, left * portions[i] // mass), spare)
            holding[i] = holding[i] + more
            spare = spare - more
    return np.array([limit] + holding)


def uneven_parts(own_key, amount, total, bound, slope):
    if amount == 2:
        one = jax.random.randint(own_key, (), max(1, total - bound), min(bound, total - 1) + 1)
        return jnp.stack([one, total - one])
    lengths = jnp.asarray(profile(amount, total, bound, slope), jnp.int32)
    couples = (amount - 1) // 2
    giver, taker = lengths[1:1 + 2 * couples:2], lengths[2:2 + 2 * couples:2]
    slack = jnp.minimum(giver - 1, bound - taker)
    shifted = jax.random.randint(jax.random.fold_in(own_key, 1), (couples,), 0, 1 << 20) % (slack + 1)
    lengths = lengths.at[1:1 + 2 * couples:2].set(giver - shifted).at[2:2 + 2 * couples:2].set(taker + shifted)
    return lengths[jax.random.permutation(jax.random.fold_in(own_key, 2), amount)]


def setup_inputs(seed: int = 0) -> dict:
    splits = jax.random.split(jax.random.key(seed), 10)
    return {
        "queries": draw_queries(jax.random.fold_in(splits[9], 71), 0),
        "suffix_kv": draw_suffix_kv(jax.random.fold_in(splits[9], 71), 0),
        "suffix_len": uneven_parts(splits[2], REQS, REQS * SUFFIX_TOKENS * 5 // 8, SUFFIX_TOKENS, 0).astype(jnp.int32),
        "sys_kv": draw_sys_kv(jax.random.fold_in(splits[9], 71), 0),
        "doc_kv": draw_doc_kv(jax.random.fold_in(splits[9], 71), 0),
        "doc_home": jax.random.permutation(splits[5], DOCS).astype(jnp.int32),
        "doc_of": draw_doc_of(jax.random.fold_in(splits[9], 71), 0),
        "conv_kv": draw_conv_kv(jax.random.fold_in(splits[9], 71), 0),
        "conv_of": draw_conv_of(jax.random.fold_in(splits[9], 71), 0),
    }


def settle(values):
    return lax.optimization_barrier(values.astype(jnp.bfloat16)).astype(jnp.float32)

def attend(query_rows, cache, valid):
    depth = query_rows.shape[-1]
    scale = 1.0 / math.sqrt(depth)
    keys = cache[..., :depth].astype(jnp.float32)
    values = cache[..., depth:].astype(jnp.float32)
    scores = jnp.einsum('brhgd,blhd->bhgrl', query_rows.astype(jnp.float32), keys, precision=lax.Precision.HIGHEST) * scale
    if valid is not None:
        scores = jnp.where(valid, scores, -1e+30)
    top = lax.optimization_barrier(jnp.max(scores, axis=-1, keepdims=True))
    expo = jnp.exp(scores - top)
    total = lax.optimization_barrier(jnp.sum(expo, axis=-1))
    weights = settle(expo)
    mixed = jnp.einsum('bhgrl,blhd->brhgd', weights, values, precision=lax.Precision.HIGHEST)
    total_rows = jnp.transpose(total, (0, 3, 1, 2))
    top_rows = jnp.transpose(top[..., 0], (0, 3, 1, 2))
    return (mixed / total_rows[..., None], top_rows + jnp.log(total_rows))

def blend(parts):
    top = reduce(jnp.maximum, [part[1] for part in parts])
    weights = [jnp.exp(part[1] - top) for part in parts]
    upper = reduce(jnp.add, [weight[..., None] * part[0] for weight, part in zip(weights, parts)])
    lower = reduce(jnp.add, weights)
    return upper / lower[..., None]

def reference(queries, suffix_kv, suffix_len, sys_kv, doc_kv, doc_home, doc_of, conv_kv, conv_of):
    head_group = QUERY_HEADS // KEY_VALUE_HEADS
    positions = jnp.arange(SUFFIX_TOKENS, dtype=jnp.int32)
    causal = positions[:, None] >= positions[None, :]

    def single(token_index):
        query_rows = queries[token_index].reshape(1, SUFFIX_TOKENS, KEY_VALUE_HEADS, head_group, HEAD_SIZE)
        system = attend(query_rows, sys_kv[None], None)
        doc_mixed, paper_highest_entries = attend(query_rows, doc_kv[doc_home[doc_of[token_index]]][None], None)
        passage_text = (settle(doc_mixed), paper_highest_entries)
        talk = attend(query_rows, conv_kv[conv_of[token_index]][None], None)
        own = attend(query_rows, suffix_kv[token_index][None], causal)
        merged = blend([system, passage_text, talk, own])[0]
        live = positions < suffix_len[token_index]
        merged = jnp.where(live[:, None, None, None], merged, 0.0)
        return merged.reshape(SUFFIX_TOKENS, QUERY_HEADS * HEAD_SIZE).astype(jnp.bfloat16)
    bunch = math.gcd(REQS, 16)

    def several(first):
        return jax.vmap(single)(first + jnp.arange(bunch, dtype=jnp.int32))
    firsts = jnp.arange(REQS // bunch, dtype=jnp.int32) * bunch
    return lax.map(several, firsts).reshape(REQS, SUFFIX_TOKENS, QUERY_HEADS * HEAD_SIZE)
```

```python
import functools
import math

import jax
import jax.numpy as jnp
from jax import lax
from jax.experimental import pallas as pl
from jax.experimental.pallas import tpu as pltpu
from jax.sharding import PartitionSpec as P

MESH = pl.DeviceIdType.MESH
F32 = jnp.float32
BF16 = jnp.bfloat16

NY, NZ, NT = 4, 8, 8
REQ, SUF, HEADS, DEPTH = 32, 16, 8, 128
GROUPS = REQ // 2
ROWS = 2 * SUF * HEADS
DOC, CONV, SYS_Y = 1024, 256, 128
HALF = DOC // 2
LOG2E = math.log2(math.e)
SCALE2 = LOG2E / math.sqrt(DEPTH)

SLOT_A, SLOT_B, GRP_A, GRP_B, GRP_SLOT, REQ_AT = 0, 32, 64, 80, 96, 112
PLAN = 256

STAGES = ((0, 1), (1, 2), (3, 2), (5, 2), (7, 1))
PLACE_REL = (0, 1, 7, 2, 6, 3, 5, 4)


def plan_kernel(home_ref, doc_ref, conv_ref, out_ref, count_ref):
    kv = lax.axis_index("kv")
    y, z = kv // NZ, kv % NZ
    for i in range(PLAN):
        if i < 64:
            out_ref[i] = 0
    for i in range(GROUPS):
        count_ref[i] = 0

    def step(r, carry):
        group = conv_ref[r] % GROUPS
        holder = home_ref[doc_ref[r]]
        dy = lax.rem(holder // NZ - y + NY, NY)
        rel = lax.rem(holder % NZ - z + NZ, NZ)
        place = jnp.where(rel == 0, 0, jnp.where(rel <= NZ // 2, 2 * rel - 1, 2 * (NZ - rel)))
        slot = dy * NZ + place
        seen = count_ref[group]
        count_ref[group] = seen + 1
        out_ref[SLOT_A + slot + 32 * seen] = r
        out_ref[GRP_A + group + 16 * seen] = r
        out_ref[GRP_SLOT + group] = slot
        out_ref[REQ_AT + r] = group * 2 + seen
        return carry

    lax.fori_loop(0, REQ, step, 0)


def scores(keys, rows):
    return lax.dot_general(keys, rows, (((1,), (1,)), ((), ())), preferred_element_type=F32)


def mix(values, weights):
    return lax.dot_general(values, weights, (((0,), (0,)), ((), ())), preferred_element_type=F32)


def mix_t(values_t, weights):
    return lax.dot_general(values_t, weights, (((1,), (0,)), ((), ())), preferred_element_type=F32)


def main_kernel(
    plan, lens, q_hbm, suf_hbm, sys_hbm, doc_hbm, conv_hbm, out_hbm,
    q_ref, suf_ref, conv_ref, docs, sysb, qs, qin, gq, vt, sysvt, ret_o, ret_l, d_o, d_l,
    l_acc, l_m, l_t, res, outst,
    in_sem, doc_ss, doc_rs, sys_ss, sys_rs, sysy_ss, sysy_rs, q_ss, q_rs, o_ss, o_rs, e_ss, e_rs,
    x_ss, x_rs,
):
    kv, tp = lax.axis_index("kv"), lax.axis_index("tp")
    y, z = kv // NZ, kv % NZ
    z_right = y * NZ + lax.rem(z + 1, NZ)
    z_left = y * NZ + lax.rem(z + NZ - 1, NZ)

    def y_peer(k):
        return lax.rem(y + k, NY) * NZ + z

    def t_peer(k):
        return lax.rem(tp + k, NT)

    barrier = pltpu.get_barrier_semaphore()
    peers = [(z_right, tp), (z_left, tp)]
    peers += [(y_peer(k), tp) for k in range(1, NY)]
    peers += [(kv, t_peer(k)) for k in range(1, NT)]
    loads = [
        pltpu.make_async_copy(q_hbm, q_ref, in_sem.at[0]),
        pltpu.make_async_copy(sys_hbm, sysb.at[0, pl.ds(0, 32)], in_sem.at[1]),
        pltpu.make_async_copy(doc_hbm.at[0], docs.at[0], in_sem.at[2]),
        pltpu.make_async_copy(suf_hbm, suf_ref, in_sem.at[3]),
        pltpu.make_async_copy(conv_hbm, conv_ref, in_sem.at[4]),
    ]
    for load in loads:
        load.start()
    for peer in peers:
        pl.semaphore_signal(barrier, inc=1, device_id=peer, device_id_type=MESH)
    pl.semaphore_wait(barrier, len(peers))

    def remote(src, dst, ss, rs, peer):
        return pltpu.make_async_remote_copy(
            src_ref=src, dst_ref=dst, send_sem=ss, recv_sem=rs, device_id=peer, device_id_type=MESH
        )

    def doc_copy(way, hop, part):
        rel_src = (NZ - (hop - 1)) % NZ if way == 0 else hop - 1
        rel_dst = NZ - hop if way == 0 else hop
        rows = pl.ds(part * HALF, HALF)
        src = doc_hbm.at[0, rows] if hop == 1 else docs.at[rel_src, rows]
        peer = (z_right if way == 0 else z_left, tp)
        return remote(
            src, docs.at[rel_dst, rows], doc_ss.at[way, hop - 1, part], doc_rs.at[way, hop - 1, part], peer
        )

    def sys_copy(way, hop):
        rel_src = (NZ - (hop - 1)) % NZ if way == 0 else hop - 1
        rel_dst = NZ - hop if way == 0 else hop
        rows = pl.ds(0, SYS_Y) if hop < 4 else pl.ds(way * SYS_Y // 2, SYS_Y // 2)
        peer = (z_right if way == 0 else z_left, tp)
        return remote(
            sysb.at[rel_src, rows], sysb.at[rel_dst, rows],
            sys_ss.at[way, hop - 1], sys_rs.at[way, hop - 1], peer,
        )

    def sys_y_copy(k):
        return remote(
            sys_hbm, sysb.at[0, pl.ds(32 * (NY - k), 32)], sysy_ss.at[k - 1], sysy_rs.at[k - 1],
            (y_peer(k), tp),
        )

    def q_copy(k, stage):
        first, count = STAGES[stage]
        return remote(
            qs.at[pl.ds(k * NZ + first, count)], qin.at[pl.ds((NY - k) * NZ + first, count)],
            q_ss.at[k - 1, stage], q_rs.at[k - 1, stage], (y_peer(k), tp),
        )

    def o_copy(k, stage):
        first, count = STAGES[stage]
        return remote(
            ret_o.at[pl.ds(k * NZ + first, count)], d_o.at[pl.ds((NY - k) * NZ + first, count)],
            o_ss.at[k - 1, stage], o_rs.at[k - 1, stage], (y_peer(k), tp),
        )

    def e_copy(k, stage):
        first, count = STAGES[stage]
        return remote(
            ret_l.at[pl.ds(k * NZ + first, count)], d_l.at[pl.ds((NY - k) * NZ + first, count)],
            e_ss.at[k - 1, stage], e_rs.at[k - 1, stage], (y_peer(k), tp),
        )

    sent = []

    def start(copy):
        copy.start()
        sent.append(copy)

    def doc_hop(hop, part):
        for way in range(2):
            if hop == 4 and way != part:
                continue
            doc_copy(way, hop, part).wait_recv()
            if hop < 3 or (hop == 3 and way == part):
                start(doc_copy(way, hop + 1, part))

    def sys_hop(hop):
        for way in range(2):
            sys_copy(way, hop).wait_recv()
            if hop < 4:
                start(sys_copy(way, hop + 1))

    for way in range(2):
        start(doc_copy(way, 1, 0))
    for k in (1, 3, 2):
        start(sys_y_copy(k))

    loads[0].wait()

    def tile_rows(a, b):
        parts = []
        for h in range(HEADS):
            lanes = slice(h * DEPTH, (h + 1) * DEPTH)
            parts += [a[:, lanes], b[:, lanes]]
        return jnp.concatenate(parts, axis=0)

    def fill_out(s, carry):
        qs[s] = tile_rows(q_ref[plan[SLOT_A + s]], q_ref[plan[SLOT_B + s]])
        return carry

    def fill_own(s, carry):
        qin[s] = tile_rows(q_ref[plan[SLOT_A + s]], q_ref[plan[SLOT_B + s]])
        return carry

    def fill_group(g, carry):
        gq[g] = tile_rows(q_ref[plan[GRP_A + g]], q_ref[plan[GRP_B + g]])
        return carry

    lax.fori_loop(NZ, NY * NZ, fill_out, 0)
    for stage in range(len(STAGES)):
        for k in (1, 3, 2):
            start(q_copy(k, stage))
    loads[1].wait()
    for k in range(1, NY):
        sys_y_copy(k).wait_recv()
    for way in range(2):
        start(sys_copy(way, 1))
        start(doc_copy(way, 1, 1))
    lax.fori_loop(0, NZ, fill_own, 0)
    lax.fori_loop(0, GROUPS, fill_group, 0)

    def doc_stage(stage):
        first, count = STAGES[stage]
        for j in range(first, first + count):
            vt[j - first] = docs[PLACE_REL[j], :, DEPTH:].T

        def unit(i, carry):
            k = i + i // 2 - 2 * (i // 3)

            @pl.when(i > 0)
            def _():
                pltpu.make_async_remote_copy(
                    src_ref=qs.at[pl.ds(first, count)], dst_ref=qin.at[pl.ds(k * NZ + first, count)],
                    send_sem=q_ss.at[0, stage], recv_sem=q_rs.at[NY - 1 - k, stage],
                    device_id=(y_peer(k), tp), device_id_type=MESH,
                ).wait_recv()

            for j in range(first, first + count):
                s = scores(docs[PLACE_REL[j], :, :DEPTH], qin[k * NZ + j])
                top = jnp.max(s, axis=0, keepdims=True) * SCALE2
                e = jnp.exp2(s * SCALE2 - top)
                total = jnp.sum(e, axis=0, keepdims=True)
                o = mix_t(vt[j - first], e.astype(BF16))
                ret_o[k * NZ + j] = (o / total).astype(BF16)
                ret_l[k * NZ + j] = top + jnp.log(total) * LOG2E

            return carry

        lax.fori_loop(0, NY, unit, 0)
        for k in (1, 3, 2):
            start(o_copy(k, stage))
            start(e_copy(k, stage))
        for j in range(first, first + count):
            d_o[j] = ret_o[j]
            d_l[j] = ret_l[j]

    loads[3].wait()
    loads[4].wait()
    key_at = lax.broadcasted_iota(jnp.int32, (2 * SUF, ROWS), 0)
    row_at = lax.broadcasted_iota(jnp.int32, (2 * SUF, ROWS), 1)
    readable = ((row_at // SUF) % 2 == key_at // SUF) & (key_at % SUF <= row_at % SUF)

    def conv_unit(g, carry):
        rows = gq[g]
        suf = jnp.concatenate([suf_ref[plan[GRP_A + g]], suf_ref[plan[GRP_B + g]]], axis=0)
        s1 = scores(conv_ref[g, :, :DEPTH], rows)
        s2 = jnp.where(readable, scores(suf[:, :DEPTH], rows), -1e30)
        top = SCALE2 * jnp.maximum(
            jnp.max(s1, axis=0, keepdims=True), jnp.max(s2, axis=0, keepdims=True)
        )
        e1 = jnp.exp2(s1 * SCALE2 - top)
        e2 = jnp.exp2(s2 * SCALE2 - top)
        l_m[g] = top
        l_t[g] = jnp.sum(e1, axis=0, keepdims=True) + jnp.sum(e2, axis=0, keepdims=True)
        l_acc[g] = mix(conv_ref[g, :, DEPTH:], e1.astype(BF16)) + mix(suf[:, DEPTH:], e2.astype(BF16))
        return carry

    def sys_unit(g, carry):
        keys = sysb[:, :, :DEPTH].reshape(NZ * SYS_Y, DEPTH)
        s = scores(keys, gq[g])
        top = jnp.maximum(jnp.max(s, axis=0, keepdims=True) * SCALE2, l_m[g])
        e = jnp.exp2(s * SCALE2 - top)
        keep = jnp.exp2(l_m[g] - top)
        l_m[g] = top
        l_t[g] = l_t[g] * keep + jnp.sum(e, axis=0, keepdims=True)
        l_acc[g] = l_acc[g] * keep + mix_t(sysvt[...], e.astype(BF16))
        return carry

    lax.fori_loop(0, GROUPS, conv_unit, 0)
    doc_hop(1, 0)
    loads[2].wait()
    doc_stage(0)
    sys_hop(1)
    doc_hop(1, 1)
    doc_stage(1)
    sys_hop(2)
    doc_hop(2, 0)
    doc_hop(2, 1)
    doc_stage(2)
    sys_hop(3)
    doc_hop(3, 0)
    sys_hop(4)
    for rel in range(NZ):
        sysvt[:, rel * SYS_Y : (rel + 1) * SYS_Y] = sysb[rel, :, DEPTH:].T
    lax.fori_loop(0, GROUPS // 2, sys_unit, 0)
    doc_hop(3, 1)
    lax.fori_loop(GROUPS // 2, GROUPS, sys_unit, 0)
    doc_stage(3)
    doc_hop(4, 0)
    doc_hop(4, 1)
    doc_stage(4)
    for stage in range(len(STAGES)):
        for k in range(1, NY):
            o_copy(k, stage).wait_recv()
            e_copy(k, stage).wait_recv()

    def join(g, carry):
        slot = plan[GRP_SLOT + g]
        lse = d_l[slot]
        top = jnp.maximum(lse, l_m[g])
        w_doc = jnp.exp2(lse - top)
        w_loc = jnp.exp2(l_m[g] - top)
        upper = w_doc * d_o[slot].astype(F32) + w_loc * l_acc[g]
        out = (upper / (w_doc + w_loc * l_t[g])).T.astype(BF16)
        for h in range(HEADS):
            for p in range(2):
                first = (h * 2 + p) * SUF
                res[g * 2 + p, :, h * DEPTH : (h + 1) * DEPTH] = out[first : first + SUF]
        return carry

    lax.fori_loop(0, GROUPS, join, 0)
    token = lax.broadcasted_iota(jnp.int32, (SUF, HEADS * DEPTH), 0)

    def place(r, carry):
        value = res[plan[REQ_AT + r]]
        outst[r] = jnp.where(token < lens[r], value, jnp.zeros_like(value))
        return carry

    lax.fori_loop(0, REQ, place, 0)
    share = REQ // NT
    lanes = pl.ds(pl.multiple_of(tp * HEADS * DEPTH, 128), HEADS * DEPTH)

    def x_copy(k):
        return remote(
            outst.at[pl.ds(t_peer(k) * share, share)], out_hbm.at[:, :, lanes],
            x_ss.at[k - 1], x_rs.at[k - 1], (kv, t_peer(k)),
        )

    own = pltpu.make_async_copy(
        outst.at[pl.ds(tp * share, share)], out_hbm.at[:, :, lanes], in_sem.at[0]
    )
    for k in (4, 3, 5, 2, 6, 1, 7):
        start(x_copy(k))
    own.start()
    for copy in sent:
        copy.wait_send()
    own.wait()
    for k in range(1, NT):
        x_copy(k).wait_recv()


def on_device(queries, suffix_kv, suffix_len, sys_kv, doc_kv, doc_home, doc_of, conv_kv, conv_of):
    smem = pl.BlockSpec(memory_space=pltpu.SMEM)
    hbm = pl.BlockSpec(memory_space=pl.ANY)
    plan = pl.pallas_call(
        plan_kernel,
        out_shape=jax.ShapeDtypeStruct((PLAN,), jnp.int32),
        in_specs=[smem] * 3,
        out_specs=smem,
        scratch_shapes=[pltpu.SMEM((GROUPS,), jnp.int32)],
        name="plan",
    )(doc_home, doc_of, conv_of)
    dma = pltpu.SemaphoreType.DMA
    stages = len(STAGES)
    return pl.pallas_call(
        main_kernel,
        out_shape=jax.ShapeDtypeStruct((REQ // NT, SUF, NT * HEADS * DEPTH), BF16),
        in_specs=[smem] * 2 + [hbm] * 5,
        out_specs=hbm,
        scratch_shapes=[
            pltpu.VMEM((REQ, SUF, HEADS * DEPTH), BF16),
            pltpu.VMEM((REQ, SUF, 2 * DEPTH), BF16),
            pltpu.VMEM((GROUPS, CONV, 2 * DEPTH), BF16),
            pltpu.VMEM((NZ, DOC, 2 * DEPTH), BF16),
            pltpu.VMEM((NZ, SYS_Y, 2 * DEPTH), BF16),
            pltpu.VMEM((NY * NZ, ROWS, DEPTH), BF16),
            pltpu.VMEM((NY * NZ, ROWS, DEPTH), BF16),
            pltpu.VMEM((GROUPS, ROWS, DEPTH), BF16),
            pltpu.VMEM((2, DEPTH, DOC), BF16),
            pltpu.VMEM((DEPTH, NZ * SYS_Y), BF16),
            pltpu.VMEM((NY * NZ, DEPTH, ROWS), BF16),
            pltpu.VMEM((NY * NZ, 1, ROWS), F32),
            pltpu.VMEM((NY * NZ, DEPTH, ROWS), BF16),
            pltpu.VMEM((NY * NZ, 1, ROWS), F32),
            pltpu.VMEM((GROUPS, DEPTH, ROWS), F32),
            pltpu.VMEM((GROUPS, 1, ROWS), F32),
            pltpu.VMEM((GROUPS, 1, ROWS), F32),
            pltpu.VMEM((REQ, SUF, HEADS * DEPTH), BF16),
            pltpu.VMEM((REQ, SUF, HEADS * DEPTH), BF16),
            dma((5,)),
            dma((2, 4, 2)), dma((2, 4, 2)),
            dma((2, 4)), dma((2, 4)),
            dma((3,)), dma((3,)),
            dma((3, stages)), dma((3, stages)),
            dma((3, stages)), dma((3, stages)),
            dma((3, stages)), dma((3, stages)),
            dma((7,)), dma((7,)),
        ],
        compiler_params=pltpu.CompilerParams(
            collective_id=0, has_side_effects=True, vmem_limit_bytes=56 << 20
        ),
        name="cascade",
    )(
        plan,
        suffix_len,
        queries,
        suffix_kv.reshape(REQ, SUF, 2 * DEPTH),
        sys_kv.reshape(32, 2 * DEPTH),
        doc_kv.reshape(1, DOC, 2 * DEPTH),
        conv_kv.reshape(GROUPS, CONV, 2 * DEPTH),
    )


def solution(mesh):
    placed = (
        P("kv", None, "tp"),
        P("kv", None, "tp", None),
        P("kv"),
        P("kv", "tp", None),
        P("kv", None, "tp", None),
        P(),
        P("kv"),
        P("kv", None, "tp", None),
        P("kv"),
    )
    return jax.shard_map(
        on_device,
        mesh=mesh,
        in_specs=placed,
        out_specs=P(("kv", "tp"), None, None),
        check_vma=False,
    )
```

```python
import functools
import math

import jax
import jax.numpy as jnp
from jax import lax
from jax.experimental import pallas as pl
from jax.experimental.pallas import tpu as pltpu
from jax.sharding import PartitionSpec as P

MESH = pl.DeviceIdType.MESH
F32 = jnp.float32
BF16 = jnp.bfloat16

NY, NZ, NT = 4, 8, 8
REQ, SUF, HEADS, DEPTH = 32, 16, 8, 128
GROUPS = REQ // 2
ROWS = 2 * SUF * HEADS
DOC, CONV, SYS_Y = 1024, 256, 128
HALF = DOC // 2
LOG2E = math.log2(math.e)
SCALE2 = LOG2E / math.sqrt(DEPTH)

SLOT_A, SLOT_B, GRP_A, GRP_B, GRP_SLOT, REQ_AT = 0, 32, 64, 80, 96, 112
PLAN = 256

STAGES = ((0, 1), (1, 2), (3, 2), (5, 2), (7, 1))
PLACE_REL = (0, 1, 7, 2, 6, 3, 5, 4)


def plan_kernel(home_ref, doc_ref, conv_ref, out_ref, count_ref):
    kv = lax.axis_index("kv")
    y, z = kv // NZ, kv % NZ
    for i in range(PLAN):
        if i < 64:
            out_ref[i] = 0
    for i in range(GROUPS):
        count_ref[i] = 0

    def step(r, carry):
        group = conv_ref[r] % GROUPS
        holder = home_ref[doc_ref[r]]
        dy = lax.rem(holder // NZ - y + NY, NY)
        rel = lax.rem(holder % NZ - z + NZ, NZ)
        place = jnp.where(rel == 0, 0, jnp.where(rel <= NZ // 2, 2 * rel - 1, 2 * (NZ - rel)))
        slot = dy * NZ + place
        seen = count_ref[group]
        count_ref[group] = seen + 1
        out_ref[SLOT_A + slot + 32 * seen] = r
        out_ref[GRP_A + group + 16 * seen] = r
        out_ref[GRP_SLOT + group] = slot
        out_ref[REQ_AT + r] = group * 2 + seen
        return carry

    lax.fori_loop(0, REQ, step, 0)


def scores(keys, rows):
    return lax.dot_general(keys, rows, (((1,), (1,)), ((), ())), preferred_element_type=F32)


def mix(values, weights):
    return lax.dot_general(values, weights, (((0,), (0,)), ((), ())), preferred_element_type=F32)


def mix_t(values_t, weights):
    return lax.dot_general(values_t, weights, (((1,), (0,)), ((), ())), preferred_element_type=F32)


def main_kernel(
    plan, lens, q_hbm, suf_hbm, sys_hbm, doc_hbm, conv_hbm, out_hbm,
    q_ref, suf_ref, conv_ref, docs, sysb, qs, qin, gq, vt, sysvt, ret_o, ret_l, d_o, d_l,
    l_acc, l_m, l_t, res, outst, s_a, s_b,
    in_sem, doc_ss, doc_rs, sys_ss, sys_rs, sysy_ss, sysy_rs, q_ss, q_rs, o_ss, o_rs, e_ss, e_rs,
    x_ss, x_rs,
):
    kv, tp = lax.axis_index("kv"), lax.axis_index("tp")
    y, z = kv // NZ, kv % NZ
    z_right = y * NZ + lax.rem(z + 1, NZ)
    z_left = y * NZ + lax.rem(z + NZ - 1, NZ)

    def y_peer(k):
        return lax.rem(y + k, NY) * NZ + z

    def t_peer(k):
        return lax.rem(tp + k, NT)

    barrier = pltpu.get_barrier_semaphore()
    peers = [(z_right, tp), (z_left, tp)]
    peers += [(y_peer(k), tp) for k in range(1, NY)]
    peers += [(kv, t_peer(k)) for k in range(1, NT)]
    loads = [
        pltpu.make_async_copy(q_hbm, q_ref, in_sem.at[0]),
        pltpu.make_async_copy(sys_hbm, sysb.at[0, pl.ds(0, 32)], in_sem.at[1]),
        pltpu.make_async_copy(doc_hbm.at[0], docs.at[0], in_sem.at[2]),
        pltpu.make_async_copy(suf_hbm, suf_ref, in_sem.at[3]),
        pltpu.make_async_copy(conv_hbm, conv_ref, in_sem.at[4]),
    ]
    for load in loads:
        load.start()
    for peer in peers:
        pl.semaphore_signal(barrier, inc=1, device_id=peer, device_id_type=MESH)
    pl.semaphore_wait(barrier, len(peers))

    def remote(src, dst, ss, rs, peer):
        return pltpu.make_async_remote_copy(
            src_ref=src, dst_ref=dst, send_sem=ss, recv_sem=rs, device_id=peer, device_id_type=MESH
        )

    def doc_copy(way, hop, part):
        rel_src = (NZ - (hop - 1)) % NZ if way == 0 else hop - 1
        rel_dst = NZ - hop if way == 0 else hop
        rows = pl.ds(part * HALF, HALF)
        src = doc_hbm.at[0, rows] if hop == 1 else docs.at[rel_src, rows]
        peer = (z_right if way == 0 else z_left, tp)
        return remote(
            src, docs.at[rel_dst, rows], doc_ss.at[way, hop - 1, part], doc_rs.at[way, hop - 1, part], peer
        )

    def sys_copy(way, hop):
        rel_src = (NZ - (hop - 1)) % NZ if way == 0 else hop - 1
        rel_dst = NZ - hop if way == 0 else hop
        rows = pl.ds(0, SYS_Y) if hop < 4 else pl.ds(way * SYS_Y // 2, SYS_Y // 2)
        peer = (z_right if way == 0 else z_left, tp)
        return remote(
            sysb.at[rel_src, rows], sysb.at[rel_dst, rows],
            sys_ss.at[way, hop - 1], sys_rs.at[way, hop - 1], peer,
        )

    def sys_y_copy(k):
        return remote(
            sys_hbm, sysb.at[0, pl.ds(32 * (NY - k), 32)], sysy_ss.at[k - 1], sysy_rs.at[k - 1],
            (y_peer(k), tp),
        )

    def q_copy(k, stage):
        first, count = STAGES[stage]
        return remote(
            qs.at[pl.ds(k * NZ + first, count)], qin.at[pl.ds((NY - k) * NZ + first, count)],
            q_ss.at[k - 1, stage], q_rs.at[k - 1, stage], (y_peer(k), tp),
        )

    def o_copy(k, stage):
        first, count = STAGES[stage]
        return remote(
            ret_o.at[pl.ds(k * NZ + first, count)], d_o.at[pl.ds((NY - k) * NZ + first, count)],
            o_ss.at[k - 1, stage], o_rs.at[k - 1, stage], (y_peer(k), tp),
        )

    def e_copy(k, stage):
        first, count = STAGES[stage]
        return remote(
            ret_l.at[pl.ds(k * NZ + first, count)], d_l.at[pl.ds((NY - k) * NZ + first, count)],
            e_ss.at[k - 1, stage], e_rs.at[k - 1, stage], (y_peer(k), tp),
        )

    sent = []

    def start(copy):
        copy.start()
        sent.append(copy)

    def doc_hop(hop, part):
        for way in range(2):
            if hop == 4 and way != part:
                continue
            doc_copy(way, hop, part).wait_recv()
            if hop < 3 or (hop == 3 and way == part):
                start(doc_copy(way, hop + 1, part))

    def sys_hop(hop):
        for way in range(2):
            sys_copy(way, hop).wait_recv()
            if hop < 4:
                start(sys_copy(way, hop + 1))

    for way in range(2):
        start(doc_copy(way, 1, 0))
    for k in (1, 3, 2):
        start(sys_y_copy(k))

    loads[0].wait()

    def tile_rows(a, b):
        parts = []
        for h in range(HEADS):
            lanes = slice(h * DEPTH, (h + 1) * DEPTH)
            parts += [a[:, lanes], b[:, lanes]]
        return jnp.concatenate(parts, axis=0)

    def fill_out(s, carry):
        qs[s] = tile_rows(q_ref[plan[SLOT_A + s]], q_ref[plan[SLOT_B + s]])
        return carry

    def fill_own(s, carry):
        qin[s] = tile_rows(q_ref[plan[SLOT_A + s]], q_ref[plan[SLOT_B + s]])
        return carry

    def fill_group(g, carry):
        gq[g] = tile_rows(q_ref[plan[GRP_A + g]], q_ref[plan[GRP_B + g]])
        return carry

    lax.fori_loop(NZ, NY * NZ, fill_out, 0)
    for stage in range(len(STAGES)):
        for k in (1, 3, 2):
            start(q_copy(k, stage))
    loads[1].wait()
    for k in range(1, NY):
        sys_y_copy(k).wait_recv()
    for way in range(2):
        start(sys_copy(way, 1))
        start(doc_copy(way, 1, 1))
    lax.fori_loop(0, NZ, fill_own, 0)
    lax.fori_loop(0, GROUPS, fill_group, 0)

    def attend(n, parts, done):
        def score(u, buf, part, top):
            first, size, score_of, _ = part
            s = score_of(u)
            buf[first : first + size] = s
            high = jnp.max(s.reshape(size // 8, 8, ROWS), axis=0)
            return high if top is None else jnp.maximum(top, high)

        def weigh(u, buf, part, top, state):
            first, size, _, mix_of = part
            e = jnp.exp2(buf[first : first + size] * SCALE2 - top)
            total = jnp.sum(e.reshape(size // 8, 8, ROWS), axis=0)
            o = mix_of(u, e.astype(BF16))
            return (o, total) if state is None else (state[0] + o, state[1] + total)

        def both(u_next, buf_next, u, buf, top):
            high = state = None
            for part in parts:
                high = score(u_next, buf_next, part, high)
                state = weigh(u, buf, part, top, state)
            done(u, state[0], jnp.sum(state[1], axis=0, keepdims=True), top)
            return jnp.max(high, axis=0, keepdims=True) * SCALE2

        def pair(i, top):
            top = both(2 * i + 1, s_b, 2 * i, s_a, top)
            return both(lax.rem(2 * i + 2, n), s_a, 2 * i + 1, s_b, top)

        high = None
        for part in parts:
            high = score(0, s_a, part, high)
        lax.fori_loop(0, n // 2, pair, jnp.max(high, axis=0, keepdims=True) * SCALE2)

    def doc_stage(stage):
        first, count = STAGES[stage]
        rel = PLACE_REL[first]
        for k in (1, 3, 2):
            q_copy(NY - k, stage).wait_recv()
        for j in range(count):
            vt[j] = docs[PLACE_REL[first + j], :, DEPTH:].T

        def place_of(u):
            return (u // count) * NZ + first + u % count

        def rel_of(u):
            return rel + (u % count) * (NZ - 2 * rel)

        def part(at):
            keys = pl.ds(at, HALF)
            return (
                at, HALF,
                lambda u: scores(docs[rel_of(u), keys, :DEPTH], qin[place_of(u)]),
                lambda u, e: mix_t(vt[u % count, :, at : at + HALF], e),
            )

        def done(u, acc, total, top):
            ret_o[place_of(u)] = (acc * (1.0 / total)).astype(BF16)
            ret_l[place_of(u)] = top + jnp.log(total) * LOG2E

        attend(NY * count, [part(0), part(HALF)], done)
        for k in (1, 3, 2):
            start(o_copy(k, stage))
            start(e_copy(k, stage))
        for j in range(first, first + count):
            d_o[j] = ret_o[j]
            d_l[j] = ret_l[j]

    loads[3].wait()
    loads[4].wait()
    key_at = lax.broadcasted_iota(jnp.int32, (2 * SUF, ROWS), 0)
    row_at = lax.broadcasted_iota(jnp.int32, (2 * SUF, ROWS), 1)
    readable = ((row_at // SUF) % 2 == key_at // SUF) & (key_at % SUF <= row_at % SUF)

    def own_tokens(g, lanes):
        return jnp.concatenate(
            [suf_ref[plan[GRP_A + g], :, lanes], suf_ref[plan[GRP_B + g], :, lanes]], axis=0
        )

    conv_parts = [
        (
            0, CONV,
            lambda g: scores(conv_ref[g, :, :DEPTH], gq[g]),
            lambda g, e: mix(conv_ref[g, :, DEPTH:], e),
        ),
        (
            CONV, 2 * SUF,
            lambda g: jnp.where(readable, scores(own_tokens(g, slice(0, DEPTH)), gq[g]), -1e30),
            lambda g, e: mix(own_tokens(g, slice(DEPTH, 2 * DEPTH)), e),
        ),
    ]

    def conv_done(g, acc, total, top):
        l_m[g] = top
        l_t[g] = total
        l_acc[g] = acc

    def sys_part(at):
        rels = pl.ds(at // SYS_Y, HALF // SYS_Y)
        return (
            at, HALF,
            lambda g: scores(sysb[rels, :, :DEPTH].reshape(HALF, DEPTH), gq[g]),
            lambda g, e: mix_t(sysvt[:, at : at + HALF], e),
        )

    def sys_done(g, acc, total, top):
        high = jnp.maximum(l_m[g], top)
        w_old = jnp.exp2(l_m[g] - high)
        w_new = jnp.exp2(top - high)
        l_m[g] = high
        l_t[g] = l_t[g] * w_old + total * w_new
        l_acc[g] = l_acc[g] * w_old + acc * w_new

    attend(GROUPS, conv_parts, conv_done)
    doc_hop(1, 0)
    loads[2].wait()
    doc_stage(0)
    sys_hop(1)
    doc_hop(1, 1)
    doc_stage(1)
    sys_hop(2)
    doc_hop(2, 0)
    doc_hop(2, 1)
    doc_stage(2)
    sys_hop(3)
    doc_hop(3, 0)
    sys_hop(4)
    for rel in range(NZ):
        sysvt[:, rel * SYS_Y : (rel + 1) * SYS_Y] = sysb[rel, :, DEPTH:].T
    attend(GROUPS, [sys_part(0), sys_part(HALF)], sys_done)
    doc_hop(3, 1)
    doc_stage(3)
    doc_hop(4, 0)
    doc_hop(4, 1)
    doc_stage(4)
    for stage in range(len(STAGES)):
        for k in range(1, NY):
            o_copy(k, stage).wait_recv()
            e_copy(k, stage).wait_recv()

    def join(g, carry):
        slot = plan[GRP_SLOT + g]
        lse = d_l[slot]
        top = jnp.maximum(lse, l_m[g])
        w_doc = jnp.exp2(lse - top)
        w_loc = jnp.exp2(l_m[g] - top)
        upper = w_doc * d_o[slot].astype(F32) + w_loc * l_acc[g]
        out = (upper / (w_doc + w_loc * l_t[g])).T.astype(BF16)
        for h in range(HEADS):
            for p in range(2):
                first = (h * 2 + p) * SUF
                res[g * 2 + p, :, h * DEPTH : (h + 1) * DEPTH] = out[first : first + SUF]
        return carry

    lax.fori_loop(0, GROUPS, join, 0)
    token = lax.broadcasted_iota(jnp.int32, (SUF, HEADS * DEPTH), 0)

    def place(r, carry):
        value = res[plan[REQ_AT + r]]
        outst[r] = jnp.where(token < lens[r], value, jnp.zeros_like(value))
        return carry

    lax.fori_loop(0, REQ, place, 0)
    share = REQ // NT
    lanes = pl.ds(pl.multiple_of(tp * HEADS * DEPTH, 128), HEADS * DEPTH)

    def x_copy(k):
        return remote(
            outst.at[pl.ds(t_peer(k) * share, share)], out_hbm.at[:, :, lanes],
            x_ss.at[k - 1], x_rs.at[k - 1], (kv, t_peer(k)),
        )

    own = pltpu.make_async_copy(
        outst.at[pl.ds(tp * share, share)], out_hbm.at[:, :, lanes], in_sem.at[0]
    )
    for k in (4, 3, 5, 2, 6, 1, 7):
        start(x_copy(k))
    own.start()
    for copy in sent:
        copy.wait_send()
    own.wait()
    for k in range(1, NT):
        x_copy(k).wait_recv()


def on_device(queries, suffix_kv, suffix_len, sys_kv, doc_kv, doc_home, doc_of, conv_kv, conv_of):
    smem = pl.BlockSpec(memory_space=pltpu.SMEM)
    hbm = pl.BlockSpec(memory_space=pl.ANY)
    plan = pl.pallas_call(
        plan_kernel,
        out_shape=jax.ShapeDtypeStruct((PLAN,), jnp.int32),
        in_specs=[smem] * 3,
        out_specs=smem,
        scratch_shapes=[pltpu.SMEM((GROUPS,), jnp.int32)],
        name="plan",
    )(doc_home, doc_of, conv_of)
    dma = pltpu.SemaphoreType.DMA
    stages = len(STAGES)
    return pl.pallas_call(
        main_kernel,
        out_shape=jax.ShapeDtypeStruct((REQ // NT, SUF, NT * HEADS * DEPTH), BF16),
        in_specs=[smem] * 2 + [hbm] * 5,
        out_specs=hbm,
        scratch_shapes=[
            pltpu.VMEM((REQ, SUF, HEADS * DEPTH), BF16),
            pltpu.VMEM((REQ, SUF, 2 * DEPTH), BF16),
            pltpu.VMEM((GROUPS, CONV, 2 * DEPTH), BF16),
            pltpu.VMEM((NZ, DOC, 2 * DEPTH), BF16),
            pltpu.VMEM((NZ, SYS_Y, 2 * DEPTH), BF16),
            pltpu.VMEM((NY * NZ, ROWS, DEPTH), BF16),
            pltpu.VMEM((NY * NZ, ROWS, DEPTH), BF16),
            pltpu.VMEM((GROUPS, ROWS, DEPTH), BF16),
            pltpu.VMEM((2, DEPTH, DOC), BF16),
            pltpu.VMEM((DEPTH, NZ * SYS_Y), BF16),
            pltpu.VMEM((NY * NZ, DEPTH, ROWS), BF16),
            pltpu.VMEM((NY * NZ, 1, ROWS), F32),
            pltpu.VMEM((NY * NZ, DEPTH, ROWS), BF16),
            pltpu.VMEM((NY * NZ, 1, ROWS), F32),
            pltpu.VMEM((GROUPS, DEPTH, ROWS), F32),
            pltpu.VMEM((GROUPS, 1, ROWS), F32),
            pltpu.VMEM((GROUPS, 1, ROWS), F32),
            pltpu.VMEM((REQ, SUF, HEADS * DEPTH), BF16),
            pltpu.VMEM((REQ, SUF, HEADS * DEPTH), BF16),
            pltpu.VMEM((DOC, ROWS), F32),
            pltpu.VMEM((DOC, ROWS), F32),
            dma((5,)),
            dma((2, 4, 2)), dma((2, 4, 2)),
            dma((2, 4)), dma((2, 4)),
            dma((3,)), dma((3,)),
            dma((3, stages)), dma((3, stages)),
            dma((3, stages)), dma((3, stages)),
            dma((3, stages)), dma((3, stages)),
            dma((7,)), dma((7,)),
        ],
        compiler_params=pltpu.CompilerParams(
            collective_id=0, has_side_effects=True, vmem_limit_bytes=56 << 20
        ),
        name="cascade",
    )(
        plan,
        suffix_len,
        queries,
        suffix_kv.reshape(REQ, SUF, 2 * DEPTH),
        sys_kv.reshape(32, 2 * DEPTH),
        doc_kv.reshape(1, DOC, 2 * DEPTH),
        conv_kv.reshape(GROUPS, CONV, 2 * DEPTH),
    )


def solution(mesh):
    placed = (
        P("kv", None, "tp"),
        P("kv", None, "tp", None),
        P("kv"),
        P("kv", "tp", None),
        P("kv", None, "tp", None),
        P(),
        P("kv"),
        P("kv", None, "tp", None),
        P("kv"),
    )
    return jax.shard_map(
        on_device,
        mesh=mesh,
        in_specs=placed,
        out_specs=P(("kv", "tp"), None, None),
        check_vma=False,
    )
```

```python
import functools
import math

import jax
import jax.numpy as jnp
from jax import lax
from jax.experimental import pallas as pl
from jax.experimental.pallas import tpu as pltpu
from jax.sharding import PartitionSpec as P

MESH = pl.DeviceIdType.MESH
F32 = jnp.float32
BF16 = jnp.bfloat16

NY, NZ, NT = 4, 8, 8
REQ, SUF, HEADS, DEPTH = 32, 16, 8, 128
GROUPS = REQ // 2
ROWS = 2 * SUF * HEADS
DOC, CONV, SYS_Y = 1024, 256, 128
HALF = DOC // 2
PARTS = 4
PIECE = DOC // PARTS
LOG2E = math.log2(math.e)
SCALE2 = LOG2E / math.sqrt(DEPTH)

SLOT_A, SLOT_B, GRP_A, GRP_B, GRP_SLOT, REQ_AT = 0, 32, 64, 80, 96, 112
PLAN = 256

STAGES = ((0, 1), (1, 2), (3, 2), (5, 2), (7, 1))
PLACE_REL = (0, 1, 7, 2, 6, 3, 5, 4)
REL_PLACE = (0, 1, 3, 5, 7, 6, 4, 2)
SYS_FIRST = 5 * SYS_Y


def plan_kernel(home_ref, doc_ref, conv_ref, out_ref, count_ref):
    kv = lax.axis_index("kv")
    y, z = kv // NZ, kv % NZ
    for i in range(64):
        out_ref[i] = 0
    for i in range(GROUPS):
        count_ref[i] = 0
    for r in range(REQ):
        group = conv_ref[r] & (GROUPS - 1)
        holder = home_ref[doc_ref[r]]
        dy = ((holder >> 3) - y) & (NY - 1)
        rel = (holder - z) & (NZ - 1)
        place = jnp.where(rel == 0, 0, jnp.where(rel <= NZ // 2, 2 * rel - 1, 2 * (NZ - rel)))
        slot = dy * NZ + place
        seen = count_ref[group]
        count_ref[group] = seen + 1
        out_ref[SLOT_A + slot + 32 * seen] = r
        out_ref[GRP_A + group + 16 * seen] = r
        out_ref[GRP_SLOT + group] = slot
        out_ref[REQ_AT + r] = group * 2 + seen


def scores(keys, rows):
    return lax.dot_general(keys, rows, (((1,), (1,)), ((), ())), preferred_element_type=F32)


def mix(values, weights):
    return lax.dot_general(values, weights, (((0,), (0,)), ((), ())), preferred_element_type=F32)


def mix_t(values_t, weights):
    return lax.dot_general(values_t, weights, (((1,), (0,)), ((), ())), preferred_element_type=F32)


def main_kernel(
    plan, lens, q_hbm, suf_hbm, sys_hbm, doc_hbm, conv_hbm, out_hbm,
    q_ref, suf_ref, conv_ref, docs, sysb, qs, qin, gq, vt, sysvt, ret_o, ret_l, d_o, d_l,
    l_acc, l_m, l_t, res, outst, s_a, s_b, p_acc, p_m, p_t,
    in_sem, doc_ss, doc_rs, sys_ss, sys_rs, sysy_ss, sysy_rs, q_ss, q_rs, o_ss, o_rs, e_ss, e_rs,
    x_ss, x_rs,
):
    kv, tp = lax.axis_index("kv"), lax.axis_index("tp")
    y, z = kv // NZ, kv % NZ
    z_right = y * NZ + lax.rem(z + 1, NZ)
    z_left = y * NZ + lax.rem(z + NZ - 1, NZ)

    def y_peer(k):
        return lax.rem(y + k, NY) * NZ + z

    def t_peer(k):
        return lax.rem(tp + k, NT)

    barrier = pltpu.get_barrier_semaphore()
    peers = [(z_right, tp), (z_left, tp)]
    peers += [(y_peer(k), tp) for k in range(1, NY)]
    peers += [(kv, t_peer(k)) for k in range(1, NT)]
    loads = [
        pltpu.make_async_copy(q_hbm, q_ref, in_sem.at[0]),
        pltpu.make_async_copy(sys_hbm, sysb.at[pl.ds(0, 32)], in_sem.at[1]),
        pltpu.make_async_copy(doc_hbm.at[0], docs.at[0], in_sem.at[2]),
        pltpu.make_async_copy(suf_hbm, suf_ref, in_sem.at[3]),
        pltpu.make_async_copy(conv_hbm, conv_ref, in_sem.at[4]),
    ]
    for load in loads:
        load.start()
    for peer in peers:
        pl.semaphore_signal(barrier, inc=1, device_id=peer, device_id_type=MESH)
    pl.semaphore_wait(barrier, len(peers))

    def remote(src, dst, ss, rs, peer):
        return pltpu.make_async_remote_copy(
            src_ref=src, dst_ref=dst, send_sem=ss, recv_sem=rs, device_id=peer, device_id_type=MESH
        )

    def doc_copy(way, hop, part):
        rel_src = (NZ - (hop - 1)) % NZ if way == 0 else hop - 1
        rel_dst = NZ - hop if way == 0 else hop
        rows = pl.ds(part * PIECE, PIECE)
        src = doc_hbm.at[0, rows] if hop == 1 else docs.at[rel_src, rows]
        peer = (z_right if way == 0 else z_left, tp)
        return remote(
            src, docs.at[rel_dst, rows], doc_ss.at[way, hop - 1, part], doc_rs.at[way, hop - 1, part], peer
        )

    def sys_copy(way, hop):
        rel_src = (NZ - (hop - 1)) % NZ if way == 0 else hop - 1
        rel_dst = NZ - hop if way == 0 else hop
        at, size = (0, SYS_Y) if hop < 4 else (way * SYS_Y // 2, SYS_Y // 2)
        peer = (z_right if way == 0 else z_left, tp)
        return remote(
            sysb.at[pl.ds(REL_PLACE[rel_src] * SYS_Y + at, size)],
            sysb.at[pl.ds(REL_PLACE[rel_dst] * SYS_Y + at, size)],
            sys_ss.at[way, hop - 1], sys_rs.at[way, hop - 1], peer,
        )

    def sys_y_copy(k):
        return remote(
            sys_hbm, sysb.at[pl.ds(32 * (NY - k), 32)], sysy_ss.at[k - 1], sysy_rs.at[k - 1],
            (y_peer(k), tp),
        )

    def q_copy(k, stage):
        first, count = STAGES[stage]
        return remote(
            qs.at[pl.ds(k * NZ + first, count)], qin.at[pl.ds((NY - k) * NZ + first, count)],
            q_ss.at[k - 1, stage], q_rs.at[k - 1, stage], (y_peer(k), tp),
        )

    def o_copy(k, stage):
        first, count = STAGES[stage]
        return remote(
            ret_o.at[pl.ds(k * NZ + first, count)], d_o.at[pl.ds((NY - k) * NZ + first, count)],
            o_ss.at[k - 1, stage], o_rs.at[k - 1, stage], (y_peer(k), tp),
        )

    def e_copy(k, stage):
        first, count = STAGES[stage]
        return remote(
            ret_l.at[pl.ds(k * NZ + first, count)], d_l.at[pl.ds((NY - k) * NZ + first, count)],
            e_ss.at[k - 1, stage], e_rs.at[k - 1, stage], (y_peer(k), tp),
        )

    sent = []

    def start(copy):
        copy.start()
        sent.append(copy)

    def doc_hop(hop, part):
        for way in range(2):
            if hop == 4 and way != part // 2:
                continue
            doc_copy(way, hop, part).wait_recv()
            if hop < 3 or (hop == 3 and way == part // 2):
                start(doc_copy(way, hop + 1, part))

    def sys_take(hop):
        for way in range(2):
            sys_copy(way, hop).wait_recv()

    def sys_pass(hop):
        for way in range(2):
            start(sys_copy(way, hop + 1))

    for way in range(2):
        start(doc_copy(way, 1, 0))
    for k in (1, 3, 2):
        start(sys_y_copy(k))

    loads[0].wait()

    def tile_rows(a, b):
        parts = []
        for h in range(HEADS):
            lanes = slice(h * DEPTH, (h + 1) * DEPTH)
            parts += [a[:, lanes], b[:, lanes]]
        return jnp.concatenate(parts, axis=0)

    def fill_own(s, carry):
        qin[s] = tile_rows(q_ref[plan[SLOT_A + s]], q_ref[plan[SLOT_B + s]])
        return carry

    def fill_group(g, carry):
        gq[g] = tile_rows(q_ref[plan[GRP_A + g]], q_ref[plan[GRP_B + g]])
        return carry

    for stage, (first, count) in enumerate(STAGES):

        def fill_out(i, carry, first=first, count=count):
            s = (1 + i // count) * NZ + first + i % count
            qs[s] = tile_rows(q_ref[plan[SLOT_A + s]], q_ref[plan[SLOT_B + s]])
            return carry

        lax.fori_loop(0, (NY - 1) * count, fill_out, 0)
        for k in (1, 3, 2):
            start(q_copy(k, stage))
    loads[1].wait()
    for k in range(1, NY):
        sys_y_copy(k).wait_recv()
    for way in range(2):
        start(sys_copy(way, 1))
    for part in range(1, PARTS):
        for way in range(2):
            start(doc_copy(way, 1, part))
    lax.fori_loop(0, NZ, fill_own, 0)
    lax.fori_loop(0, GROUPS, fill_group, 0)

    def attend(n, parts, done):
        def score(u, buf, part, top):
            first, size, score_of, _ = part
            s = score_of(u)
            buf[first : first + size] = s
            high = jnp.max(s.reshape(size // 8, 8, ROWS), axis=0)
            return high if top is None else jnp.maximum(top, high)

        def weigh(u, buf, part, top, state):
            first, size, _, mix_of = part
            e = jnp.exp2(buf[first : first + size] * SCALE2 - top)
            total = jnp.sum(e.reshape(size // 8, 8, ROWS), axis=0)
            o = mix_of(u, e.astype(BF16))
            return (o, total) if state is None else (state[0] + o, state[1] + total)

        def both(u_next, buf_next, u, buf, top):
            high = state = None
            for part in parts:
                high = score(u_next, buf_next, part, high)
                state = weigh(u, buf, part, top, state)
            done(u, state[0], jnp.sum(state[1], axis=0, keepdims=True), top)
            return jnp.max(high, axis=0, keepdims=True) * SCALE2

        def pair(i, top):
            top = both(2 * i + 1, s_b, 2 * i, s_a, top)
            return both(lax.rem(2 * i + 2, n), s_a, 2 * i + 1, s_b, top)

        high = None
        for part in parts:
            high = score(0, s_a, part, high)
        lax.fori_loop(0, n // 2, pair, jnp.max(high, axis=0, keepdims=True) * SCALE2)

    def doc_stage(stage):
        first, count = STAGES[stage]
        rel = PLACE_REL[first]
        for k in (1, 3, 2):
            q_copy(NY - k, stage).wait_recv()
        for j in range(count):
            vt[j] = docs[PLACE_REL[first + j], :, DEPTH:].T

        def place_of(u):
            return (u // count) * NZ + first + u % count

        def rel_of(u):
            return rel + (u % count) * (NZ - 2 * rel)

        def part(at):
            keys = pl.ds(at, HALF)
            return (
                at, HALF,
                lambda u: scores(docs[rel_of(u), keys, :DEPTH], qin[place_of(u)]),
                lambda u, e: mix_t(vt[u % count, :, at : at + HALF], e),
            )

        def done(u, acc, total, top):
            ret_o[place_of(u)] = (acc * (1.0 / total)).astype(BF16)
            ret_l[place_of(u)] = top + jnp.log(total) * LOG2E

        attend(NY * count, [part(0), part(HALF)], done)
        send_back(stage)

    def send_back(stage):
        first, count = STAGES[stage]
        for k in (1, 3, 2):
            start(o_copy(k, stage))
            start(e_copy(k, stage))
        for j in range(first, first + count):
            d_o[j] = ret_o[j]
            d_l[j] = ret_l[j]

    def last_stage():
        stage = len(STAGES) - 1
        first, rel = STAGES[stage][0], PLACE_REL[STAGES[stage][0]]
        for k in (1, 3, 2):
            q_copy(NY - k, stage).wait_recv()

        def part(at):
            keys = pl.ds(at, PIECE)
            return (
                at, PIECE,
                lambda u: scores(docs[rel, keys, :DEPTH], qin[u * NZ + first]),
                lambda u, e: mix_t(vt[0, :, at : at + PIECE], e),
            )

        def hold(u, acc, total, top):
            p_m[u] = top
            p_t[u] = total
            p_acc[u] = acc

        def done(u, acc, total, top):
            high = jnp.maximum(p_m[u], top)
            w_old = jnp.exp2(p_m[u] - high)
            w_new = jnp.exp2(top - high)
            total = p_t[u] * w_old + total * w_new
            ret_o[u * NZ + first] = ((p_acc[u] * w_old + acc * w_new) * (1.0 / total)).astype(BF16)
            ret_l[u * NZ + first] = high + jnp.log(total) * LOG2E

        for pieces, finish in (((0, 2), hold), ((1, 3), done)):
            for piece in pieces:
                at = piece * PIECE
                doc_hop(4, piece)
                vt[0, :, at : at + PIECE] = docs[rel, at : at + PIECE, DEPTH:].T
            attend(NY, [part(piece * PIECE) for piece in pieces], finish)
        send_back(stage)

    loads[3].wait()
    loads[4].wait()
    key_at = lax.broadcasted_iota(jnp.int32, (2 * SUF, ROWS), 0)
    row_at = lax.broadcasted_iota(jnp.int32, (2 * SUF, ROWS), 1)
    readable = ((row_at // SUF) % 2 == key_at // SUF) & (key_at % SUF <= row_at % SUF)

    def own_tokens(g, lanes):
        return jnp.concatenate(
            [suf_ref[plan[GRP_A + g], :, lanes], suf_ref[plan[GRP_B + g], :, lanes]], axis=0
        )

    conv_parts = [
        (
            0, CONV,
            lambda g: scores(conv_ref[g, :, :DEPTH], gq[g]),
            lambda g, e: mix(conv_ref[g, :, DEPTH:], e),
        ),
        (
            CONV, 2 * SUF,
            lambda g: jnp.where(readable, scores(own_tokens(g, slice(0, DEPTH)), gq[g]), -1e30),
            lambda g, e: mix(own_tokens(g, slice(DEPTH, 2 * DEPTH)), e),
        ),
    ]

    def conv_done(g, acc, total, top):
        l_m[g] = top
        l_t[g] = total
        l_acc[g] = acc

    def sys_part(at, size):
        keys = pl.ds(at, size)
        return (
            at, size,
            lambda g: scores(sysb[keys, :DEPTH], gq[g]),
            lambda g, e: mix_t(sysvt[:, at : at + size], e),
        )

    def turn_sys(first, last):
        for place in range(first, last):
            at = place * SYS_Y
            sysvt[:, at : at + SYS_Y] = sysb[at : at + SYS_Y, DEPTH:].T

    def sys_done(g, acc, total, top):
        high = jnp.maximum(l_m[g], top)
        w_old = jnp.exp2(l_m[g] - high)
        w_new = jnp.exp2(top - high)
        l_m[g] = high
        l_t[g] = l_t[g] * w_old + total * w_new
        l_acc[g] = l_acc[g] * w_old + acc * w_new

    attend(GROUPS, conv_parts, conv_done)
    sys_take(1)
    sys_pass(1)
    doc_hop(1, 0)
    loads[2].wait()
    doc_stage(0)
    doc_hop(1, 1)
    doc_hop(1, 2)
    doc_hop(1, 3)
    doc_stage(1)
    sys_take(2)
    doc_hop(2, 0)
    turn_sys(0, 5)
    attend(GROUPS, [sys_part(0, 384), sys_part(384, SYS_FIRST - 384)], sys_done)
    doc_hop(2, 1)
    doc_hop(2, 2)
    doc_hop(2, 3)
    sys_pass(2)
    doc_stage(2)
    for part in range(PARTS):
        doc_hop(3, part)
    sys_take(3)
    sys_pass(3)
    doc_stage(3)
    last_stage()
    sys_take(4)
    turn_sys(5, 8)
    attend(GROUPS, [sys_part(SYS_FIRST, NZ * SYS_Y - SYS_FIRST)], sys_done)
    for stage in range(len(STAGES)):
        for k in range(1, NY):
            o_copy(k, stage).wait_recv()
            e_copy(k, stage).wait_recv()

    def join(g, carry):
        slot = plan[GRP_SLOT + g]
        lse = d_l[slot]
        top = jnp.maximum(lse, l_m[g])
        w_doc = jnp.exp2(lse - top)
        w_loc = jnp.exp2(l_m[g] - top)
        upper = w_doc * d_o[slot].astype(F32) + w_loc * l_acc[g]
        out = (upper / (w_doc + w_loc * l_t[g])).T.astype(BF16)
        for h in range(HEADS):
            for p in range(2):
                first = (h * 2 + p) * SUF
                res[g * 2 + p, :, h * DEPTH : (h + 1) * DEPTH] = out[first : first + SUF]
        return carry

    lax.fori_loop(0, GROUPS, join, 0)
    token = lax.broadcasted_iota(jnp.int32, (SUF, HEADS * DEPTH), 0)

    share = REQ // NT
    lanes = pl.ds(pl.multiple_of(tp * HEADS * DEPTH, 128), HEADS * DEPTH)

    def x_copy(k):
        return remote(
            outst.at[pl.ds(t_peer(k) * share, share)], out_hbm.at[:, :, lanes],
            x_ss.at[k - 1], x_rs.at[k - 1], (kv, t_peer(k)),
        )

    own = pltpu.make_async_copy(
        outst.at[pl.ds(tp * share, share)], out_hbm.at[:, :, lanes], in_sem.at[0]
    )
    for k in (4, 3, 5, 2, 6, 1, 7, 0):
        for i in range(share):
            r = t_peer(k) * share + i
            value = res[plan[REQ_AT + r]]
            outst[r] = jnp.where(token < lens[r], value, jnp.zeros_like(value))
        if k:
            start(x_copy(k))
        else:
            own.start()
    for copy in sent:
        copy.wait_send()
    own.wait()
    for k in range(1, NT):
        x_copy(k).wait_recv()


def on_device(queries, suffix_kv, suffix_len, sys_kv, doc_kv, doc_home, doc_of, conv_kv, conv_of):
    smem = pl.BlockSpec(memory_space=pltpu.SMEM)
    hbm = pl.BlockSpec(memory_space=pl.ANY)
    plan = pl.pallas_call(
        plan_kernel,
        out_shape=jax.ShapeDtypeStruct((PLAN,), jnp.int32),
        in_specs=[smem] * 3,
        out_specs=smem,
        scratch_shapes=[pltpu.SMEM((GROUPS,), jnp.int32)],
        name="plan",
    )(doc_home, doc_of, conv_of)
    dma = pltpu.SemaphoreType.DMA
    stages = len(STAGES)
    return pl.pallas_call(
        main_kernel,
        out_shape=jax.ShapeDtypeStruct((REQ // NT, SUF, NT * HEADS * DEPTH), BF16),
        in_specs=[smem] * 2 + [hbm] * 5,
        out_specs=hbm,
        scratch_shapes=[
            pltpu.VMEM((REQ, SUF, HEADS * DEPTH), BF16),
            pltpu.VMEM((REQ, SUF, 2 * DEPTH), BF16),
            pltpu.VMEM((GROUPS, CONV, 2 * DEPTH), BF16),
            pltpu.VMEM((NZ, DOC, 2 * DEPTH), BF16),
            pltpu.VMEM((NZ * SYS_Y, 2 * DEPTH), BF16),
            pltpu.VMEM((NY * NZ, ROWS, DEPTH), BF16),
            pltpu.VMEM((NY * NZ, ROWS, DEPTH), BF16),
            pltpu.VMEM((GROUPS, ROWS, DEPTH), BF16),
            pltpu.VMEM((2, DEPTH, DOC), BF16),
            pltpu.VMEM((DEPTH, NZ * SYS_Y), BF16),
            pltpu.VMEM((NY * NZ, DEPTH, ROWS), BF16),
            pltpu.VMEM((NY * NZ, 1, ROWS), F32),
            pltpu.VMEM((NY * NZ, DEPTH, ROWS), BF16),
            pltpu.VMEM((NY * NZ, 1, ROWS), F32),
            pltpu.VMEM((GROUPS, DEPTH, ROWS), F32),
            pltpu.VMEM((GROUPS, 1, ROWS), F32),
            pltpu.VMEM((GROUPS, 1, ROWS), F32),
            pltpu.VMEM((REQ, SUF, HEADS * DEPTH), BF16),
            pltpu.VMEM((REQ, SUF, HEADS * DEPTH), BF16),
            pltpu.VMEM((DOC, ROWS), F32),
            pltpu.VMEM((DOC, ROWS), F32),
            pltpu.VMEM((NY, DEPTH, ROWS), F32),
            pltpu.VMEM((NY, 1, ROWS), F32),
            pltpu.VMEM((NY, 1, ROWS), F32),
            dma((5,)),
            dma((2, 4, PARTS)), dma((2, 4, PARTS)),
            dma((2, 4)), dma((2, 4)),
            dma((3,)), dma((3,)),
            dma((3, stages)), dma((3, stages)),
            dma((3, stages)), dma((3, stages)),
            dma((3, stages)), dma((3, stages)),
            dma((7,)), dma((7,)),
        ],
        compiler_params=pltpu.CompilerParams(
            collective_id=0, has_side_effects=True, vmem_limit_bytes=56 << 20
        ),
        name="cascade",
    )(
        plan,
        suffix_len,
        queries,
        suffix_kv.reshape(REQ, SUF, 2 * DEPTH),
        sys_kv.reshape(32, 2 * DEPTH),
        doc_kv.reshape(1, DOC, 2 * DEPTH),
        conv_kv.reshape(GROUPS, CONV, 2 * DEPTH),
    )


def solution(mesh):
    placed = (
        P("kv", None, "tp"),
        P("kv", None, "tp", None),
        P("kv"),
        P("kv", "tp", None),
        P("kv", None, "tp", None),
        P(),
        P("kv"),
        P("kv", None, "tp", None),
        P("kv"),
    )
    return jax.shard_map(
        on_device,
        mesh=mesh,
        in_specs=placed,
        out_specs=P(("kv", "tp"), None, None),
        check_vma=False,
    )
```

```python
import functools
import math

import jax
import jax.numpy as jnp
from jax import lax
from jax.experimental import pallas as pl
from jax.experimental.pallas import tpu as pltpu
from jax.sharding import PartitionSpec as P

MESH = pl.DeviceIdType.MESH
F32 = jnp.float32
BF16 = jnp.bfloat16

NY, NZ, NT = 4, 8, 8
REQ, SUF, HEADS, DEPTH = 32, 16, 8, 128
GROUPS = REQ // 2
ROWS = 2 * SUF * HEADS
DOC, CONV, SYS_Y = 1024, 256, 128
HALF = DOC // 2
PARTS = 4
PIECE = DOC // PARTS
LOG2E = math.log2(math.e)
SCALE2 = LOG2E / math.sqrt(DEPTH)

SLOT_A, SLOT_B, GRP_A, GRP_B, GRP_SLOT, REQ_AT = 0, 32, 64, 80, 96, 112
PLAN = 256

STAGES = ((0, 1), (1, 2), (3, 2), (5, 2), (7, 1))
PLACE_REL = (0, 1, 7, 2, 6, 3, 5, 4)
REL_PLACE = (0, 1, 3, 5, 7, 6, 4, 2)
SYS_FIRST = 5 * SYS_Y


def plan_kernel(home_ref, doc_ref, conv_ref, out_ref, count_ref):
    kv = lax.axis_index("kv")
    y, z = kv // NZ, kv % NZ
    for i in range(64):
        out_ref[i] = 0
    for i in range(GROUPS):
        count_ref[i] = 0
    for r in range(REQ):
        group = conv_ref[r] & (GROUPS - 1)
        holder = home_ref[doc_ref[r]]
        dy = ((holder >> 3) - y) & (NY - 1)
        rel = (holder - z) & (NZ - 1)
        place = jnp.where(rel == 0, 0, jnp.where(rel <= NZ // 2, 2 * rel - 1, 2 * (NZ - rel)))
        slot = dy * NZ + place
        seen = count_ref[group]
        count_ref[group] = seen + 1
        out_ref[SLOT_A + slot + 32 * seen] = r
        out_ref[GRP_A + group + 16 * seen] = r
        out_ref[GRP_SLOT + group] = slot
        out_ref[REQ_AT + r] = group * 2 + seen


def scores(keys, rows):
    return lax.dot_general(keys, rows, (((1,), (1,)), ((), ())), preferred_element_type=F32)


def mix(values, weights):
    return lax.dot_general(values, weights, (((0,), (0,)), ((), ())), preferred_element_type=F32)


def mix_t(values_t, weights):
    return lax.dot_general(values_t, weights, (((1,), (0,)), ((), ())), preferred_element_type=F32)


def main_kernel(
    plan, lens, q_hbm, suf_hbm, sys_hbm, doc_hbm, conv_hbm, out_hbm,
    q_ref, suf_ref, conv_ref, docs, sysb, qs, qin, gq, vt, sysvt, ret_o, ret_l, d_o, d_l,
    l_acc, l_m, l_t, res, outst, s_a, s_b, p_acc, p_m, p_t,
    in_sem, doc_ss, doc_rs, sys_ss, sys_rs, sysy_ss, sysy_rs, q_ss, q_rs, o_ss, o_rs, e_ss, e_rs,
    x_ss, x_rs,
):
    kv, tp = lax.axis_index("kv"), lax.axis_index("tp")
    y, z = kv // NZ, kv % NZ
    z_right = y * NZ + lax.rem(z + 1, NZ)
    z_left = y * NZ + lax.rem(z + NZ - 1, NZ)

    def y_peer(k):
        return lax.rem(y + k, NY) * NZ + z

    def t_peer(k):
        return lax.rem(tp + k, NT)

    barrier = pltpu.get_barrier_semaphore()
    peers = [(z_right, tp), (z_left, tp)]
    peers += [(y_peer(k), tp) for k in range(1, NY)]
    peers += [(kv, t_peer(k)) for k in range(1, NT)]
    loads = [
        pltpu.make_async_copy(q_hbm, q_ref, in_sem.at[0]),
        pltpu.make_async_copy(sys_hbm, sysb.at[pl.ds(0, 32)], in_sem.at[1]),
        pltpu.make_async_copy(doc_hbm.at[0], docs.at[0], in_sem.at[2]),
        pltpu.make_async_copy(suf_hbm, suf_ref, in_sem.at[3]),
        pltpu.make_async_copy(conv_hbm, conv_ref, in_sem.at[4]),
    ]
    for load in loads:
        load.start()
    for peer in peers:
        pl.semaphore_signal(barrier, inc=1, device_id=peer, device_id_type=MESH)
    pl.semaphore_wait(barrier, len(peers))

    def remote(src, dst, ss, rs, peer):
        return pltpu.make_async_remote_copy(
            src_ref=src, dst_ref=dst, send_sem=ss, recv_sem=rs, device_id=peer, device_id_type=MESH
        )

    def doc_copy(way, hop, part):
        rel_src = (NZ - (hop - 1)) % NZ if way == 0 else hop - 1
        rel_dst = NZ - hop if way == 0 else hop
        rows = pl.ds(part * PIECE, PIECE)
        src = doc_hbm.at[0, rows] if hop == 1 else docs.at[rel_src, rows]
        peer = (z_right if way == 0 else z_left, tp)
        return remote(
            src, docs.at[rel_dst, rows], doc_ss.at[way, hop - 1, part], doc_rs.at[way, hop - 1, part], peer
        )

    def sys_copy(way, hop):
        rel_src = (NZ - (hop - 1)) % NZ if way == 0 else hop - 1
        rel_dst = NZ - hop if way == 0 else hop
        at, size = (0, SYS_Y) if hop < 4 else (way * SYS_Y // 2, SYS_Y // 2)
        peer = (z_right if way == 0 else z_left, tp)
        return remote(
            sysb.at[pl.ds(REL_PLACE[rel_src] * SYS_Y + at, size)],
            sysb.at[pl.ds(REL_PLACE[rel_dst] * SYS_Y + at, size)],
            sys_ss.at[way, hop - 1], sys_rs.at[way, hop - 1], peer,
        )

    def sys_y_copy(k):
        return remote(
            sys_hbm, sysb.at[pl.ds(32 * (NY - k), 32)], sysy_ss.at[k - 1], sysy_rs.at[k - 1],
            (y_peer(k), tp),
        )

    def q_copy(k, stage):
        first, count = STAGES[stage]
        return remote(
            qs.at[pl.ds(k * NZ + first, count)], qin.at[pl.ds((NY - k) * NZ + first, count)],
            q_ss.at[k - 1, stage], q_rs.at[k - 1, stage], (y_peer(k), tp),
        )

    def o_copy(k, stage):
        first, count = STAGES[stage]
        return remote(
            ret_o.at[pl.ds(k * NZ + first, count)], d_o.at[pl.ds((NY - k) * NZ + first, count)],
            o_ss.at[k - 1, stage], o_rs.at[k - 1, stage], (y_peer(k), tp),
        )

    def e_copy(k, stage):
        first, count = STAGES[stage]
        return remote(
            ret_l.at[pl.ds(k * NZ + first, count)], d_l.at[pl.ds((NY - k) * NZ + first, count)],
            e_ss.at[k - 1, stage], e_rs.at[k - 1, stage], (y_peer(k), tp),
        )

    sent = []

    def start(copy):
        copy.start()
        sent.append(copy)

    def doc_hop(hop, part):
        for way in range(2):
            if hop == 4 and way != part // 2:
                continue
            doc_copy(way, hop, part).wait_recv()
            if hop < 3 or (hop == 3 and way == part // 2):
                start(doc_copy(way, hop + 1, part))

    def sys_take(hop):
        for way in range(2):
            sys_copy(way, hop).wait_recv()

    def sys_pass(hop):
        for way in range(2):
            start(sys_copy(way, hop + 1))

    for way in range(2):
        start(doc_copy(way, 1, 0))
    for k in (1, 3, 2):
        start(sys_y_copy(k))

    loads[0].wait()

    def tile_rows(a, b):
        parts = []
        for h in range(HEADS):
            lanes = slice(h * DEPTH, (h + 1) * DEPTH)
            parts += [a[:, lanes], b[:, lanes]]
        return jnp.concatenate(parts, axis=0)

    def fill_own(s, carry):
        qin[s] = tile_rows(q_ref[plan[SLOT_A + s]], q_ref[plan[SLOT_B + s]])
        return carry

    def fill_group(g, carry):
        gq[g] = tile_rows(q_ref[plan[GRP_A + g]], q_ref[plan[GRP_B + g]])
        return carry

    for stage, (first, count) in enumerate(STAGES):

        def fill_out(i, carry, first=first, count=count):
            s = (1 + i // count) * NZ + first + i % count
            qs[s] = tile_rows(q_ref[plan[SLOT_A + s]], q_ref[plan[SLOT_B + s]])
            return carry

        lax.fori_loop(0, (NY - 1) * count, fill_out, 0)
        for k in (1, 3, 2):
            start(q_copy(k, stage))
    loads[1].wait()
    for k in range(1, NY):
        sys_y_copy(k).wait_recv()
    for way in range(2):
        start(sys_copy(way, 1))
    for part in range(1, PARTS):
        for way in range(2):
            start(doc_copy(way, 1, part))
    lax.fori_loop(0, NZ, fill_own, 0)
    lax.fori_loop(0, GROUPS, fill_group, 0)

    def attend(n, parts, done):
        def score(u, buf, part, top):
            first, size, score_of, _ = part
            s = score_of(u)
            buf[first : first + size] = s
            high = jnp.max(s.reshape(size // 8, 8, ROWS), axis=0)
            return high if top is None else jnp.maximum(top, high)

        def weigh(u, buf, part, top, state):
            first, size, _, mix_of = part
            e = jnp.exp2(buf[first : first + size] * SCALE2 - top)
            total = jnp.sum(e.reshape(size // 8, 8, ROWS), axis=0)
            o = mix_of(u, e.astype(BF16))
            return (o, total) if state is None else (state[0] + o, state[1] + total)

        def both(u_next, buf_next, u, buf, top):
            high = state = None
            for part in parts:
                high = score(u_next, buf_next, part, high)
                state = weigh(u, buf, part, top, state)
            done(u, state[0], jnp.sum(state[1], axis=0, keepdims=True), top)
            return jnp.max(high, axis=0, keepdims=True) * SCALE2

        def pair(i, top):
            top = both(2 * i + 1, s_b, 2 * i, s_a, top)
            return both(lax.rem(2 * i + 2, n), s_a, 2 * i + 1, s_b, top)

        high = None
        for part in parts:
            high = score(0, s_a, part, high)
        lax.fori_loop(0, n // 2, pair, jnp.max(high, axis=0, keepdims=True) * SCALE2)

    def doc_stage(stage):
        first, count = STAGES[stage]
        rel = PLACE_REL[first]
        for k in (1, 3, 2):
            q_copy(NY - k, stage).wait_recv()
        for j in range(count):
            vt[j] = docs[PLACE_REL[first + j], :, DEPTH:].T

        def place_of(u):
            return source_of(u // count) * NZ + first + u % count

        def rel_of(u):
            return rel + (u % count) * (NZ - 2 * rel)

        def part(at):
            keys = pl.ds(at, HALF)
            return (
                at, HALF,
                lambda u: scores(docs[rel_of(u), keys, :DEPTH], qin[place_of(u)]),
                lambda u, e: mix_t(vt[u % count, :, at : at + HALF], e),
            )

        def done(u, acc, total, top):
            ret_o[place_of(u)] = (acc * (1.0 / total)).astype(BF16)
            ret_l[place_of(u)] = top + jnp.log(total) * LOG2E
            send_back(u, stage)

        attend(NY * count, [part(0), part(HALF)], done)
        keep_own(stage)

    def source_of(i):
        return lax.rem(i + 1, NY)

    def send_back(u, stage):
        count = STAGES[stage][1]
        k = source_of(u // count)

        @pl.when((u % count == count - 1) & (k > 0))
        def _():
            o_copy(k, stage).start()
            e_copy(k, stage).start()

    def keep_own(stage):
        first, count = STAGES[stage]
        for k in range(1, NY):
            sent.append(o_copy(k, stage))
            sent.append(e_copy(k, stage))
        for j in range(first, first + count):
            d_o[j] = ret_o[j]
            d_l[j] = ret_l[j]

    def last_stage():
        stage = len(STAGES) - 1
        first, rel = STAGES[stage][0], PLACE_REL[STAGES[stage][0]]
        for k in (1, 3, 2):
            q_copy(NY - k, stage).wait_recv()

        def part(at):
            keys = pl.ds(at, PIECE)
            return (
                at, PIECE,
                lambda u: scores(docs[rel, keys, :DEPTH], qin[source_of(u) * NZ + first]),
                lambda u, e: mix_t(vt[0, :, at : at + PIECE], e),
            )

        def hold(u, acc, total, top):
            p_m[u] = top
            p_t[u] = total
            p_acc[u] = acc

        def done(u, acc, total, top):
            high = jnp.maximum(p_m[u], top)
            w_old = jnp.exp2(p_m[u] - high)
            w_new = jnp.exp2(top - high)
            total = p_t[u] * w_old + total * w_new
            place = source_of(u) * NZ + first
            ret_o[place] = ((p_acc[u] * w_old + acc * w_new) * (1.0 / total)).astype(BF16)
            ret_l[place] = high + jnp.log(total) * LOG2E
            send_back(u, stage)

        for pieces, finish in (((0, 2), hold), ((1, 3), done)):
            for piece in pieces:
                at = piece * PIECE
                doc_hop(4, piece)
                vt[0, :, at : at + PIECE] = docs[rel, at : at + PIECE, DEPTH:].T
            attend(NY, [part(piece * PIECE) for piece in pieces], finish)
        keep_own(stage)

    loads[3].wait()
    loads[4].wait()
    key_at = lax.broadcasted_iota(jnp.int32, (2 * SUF, ROWS), 0)
    row_at = lax.broadcasted_iota(jnp.int32, (2 * SUF, ROWS), 1)
    readable = ((row_at // SUF) % 2 == key_at // SUF) & (key_at % SUF <= row_at % SUF)

    def own_tokens(g, lanes):
        return jnp.concatenate(
            [suf_ref[plan[GRP_A + g], :, lanes], suf_ref[plan[GRP_B + g], :, lanes]], axis=0
        )

    conv_parts = [
        (
            0, CONV,
            lambda g: scores(conv_ref[g, :, :DEPTH], gq[g]),
            lambda g, e: mix(conv_ref[g, :, DEPTH:], e),
        ),
        (
            CONV, 2 * SUF,
            lambda g: jnp.where(readable, scores(own_tokens(g, slice(0, DEPTH)), gq[g]), -1e30),
            lambda g, e: mix(own_tokens(g, slice(DEPTH, 2 * DEPTH)), e),
        ),
    ]

    def conv_done(g, acc, total, top):
        l_m[g] = top
        l_t[g] = total
        l_acc[g] = acc

    def sys_part(at, size):
        keys = pl.ds(at, size)
        return (
            at, size,
            lambda g: scores(sysb[keys, :DEPTH], gq[g]),
            lambda g, e: mix_t(sysvt[:, at : at + size], e),
        )

    def turn_sys(first, last):
        for place in range(first, last):
            at = place * SYS_Y
            sysvt[:, at : at + SYS_Y] = sysb[at : at + SYS_Y, DEPTH:].T

    def sys_done(g, acc, total, top):
        high = jnp.maximum(l_m[g], top)
        w_old = jnp.exp2(l_m[g] - high)
        w_new = jnp.exp2(top - high)
        l_m[g] = high
        l_t[g] = l_t[g] * w_old + total * w_new
        l_acc[g] = l_acc[g] * w_old + acc * w_new

    attend(GROUPS, conv_parts, conv_done)
    sys_take(1)
    sys_pass(1)
    doc_hop(1, 0)
    loads[2].wait()
    doc_stage(0)
    doc_hop(1, 1)
    doc_hop(1, 2)
    doc_hop(1, 3)
    doc_stage(1)
    sys_take(2)
    doc_hop(2, 0)
    turn_sys(0, 5)
    attend(GROUPS, [sys_part(0, 384), sys_part(384, SYS_FIRST - 384)], sys_done)
    doc_hop(2, 1)
    doc_hop(2, 2)
    doc_hop(2, 3)
    sys_pass(2)
    doc_stage(2)
    for part in range(PARTS):
        doc_hop(3, part)
    sys_take(3)
    sys_pass(3)
    doc_stage(3)
    last_stage()
    sys_take(4)
    turn_sys(5, 8)
    attend(GROUPS, [sys_part(SYS_FIRST, NZ * SYS_Y - SYS_FIRST)], sys_done)
    for stage in range(len(STAGES)):
        for k in range(1, NY):
            o_copy(k, stage).wait_recv()
            e_copy(k, stage).wait_recv()

    def join(g, carry):
        slot = plan[GRP_SLOT + g]
        lse = d_l[slot]
        top = jnp.maximum(lse, l_m[g])
        w_doc = jnp.exp2(lse - top)
        w_loc = jnp.exp2(l_m[g] - top)
        upper = w_doc * d_o[slot].astype(F32) + w_loc * l_acc[g]
        out = (upper / (w_doc + w_loc * l_t[g])).T.astype(BF16)
        for h in range(HEADS):
            for p in range(2):
                first = (h * 2 + p) * SUF
                res[g * 2 + p, :, h * DEPTH : (h + 1) * DEPTH] = out[first : first + SUF]
        return carry

    lax.fori_loop(0, GROUPS, join, 0)
    token = lax.broadcasted_iota(jnp.int32, (SUF, HEADS * DEPTH), 0)

    share = REQ // NT
    lanes = pl.ds(pl.multiple_of(tp * HEADS * DEPTH, 128), HEADS * DEPTH)

    def x_copy(k):
        return remote(
            outst.at[pl.ds(t_peer(k) * share, share)], out_hbm.at[:, :, lanes],
            x_ss.at[k - 1], x_rs.at[k - 1], (kv, t_peer(k)),
        )

    own = pltpu.make_async_copy(
        outst.at[pl.ds(tp * share, share)], out_hbm.at[:, :, lanes], in_sem.at[0]
    )
    for k in (4, 3, 5, 2, 6, 1, 7, 0):
        for i in range(share):
            r = t_peer(k) * share + i
            value = res[plan[REQ_AT + r]]
            outst[r] = jnp.where(token < lens[r], value, jnp.zeros_like(value))
        if k:
            start(x_copy(k))
        else:
            own.start()
    for copy in sent:
        copy.wait_send()
    own.wait()
    for k in range(1, NT):
        x_copy(k).wait_recv()


def on_device(queries, suffix_kv, suffix_len, sys_kv, doc_kv, doc_home, doc_of, conv_kv, conv_of):
    smem = pl.BlockSpec(memory_space=pltpu.SMEM)
    hbm = pl.BlockSpec(memory_space=pl.ANY)
    plan = pl.pallas_call(
        plan_kernel,
        out_shape=jax.ShapeDtypeStruct((PLAN,), jnp.int32),
        in_specs=[smem] * 3,
        out_specs=smem,
        scratch_shapes=[pltpu.SMEM((GROUPS,), jnp.int32)],
        name="plan",
    )(doc_home, doc_of, conv_of)
    dma = pltpu.SemaphoreType.DMA
    stages = len(STAGES)
    return pl.pallas_call(
        main_kernel,
        out_shape=pltpu.VMEM((REQ // NT, SUF, NT * HEADS * DEPTH), BF16),
        in_specs=[smem] * 2 + [hbm] * 5,
        out_specs=pl.BlockSpec(memory_space=pltpu.VMEM),
        scratch_shapes=[
            pltpu.VMEM((REQ, SUF, HEADS * DEPTH), BF16),
            pltpu.VMEM((REQ, SUF, 2 * DEPTH), BF16),
            pltpu.VMEM((GROUPS, CONV, 2 * DEPTH), BF16),
            pltpu.VMEM((NZ, DOC, 2 * DEPTH), BF16),
            pltpu.VMEM((NZ * SYS_Y, 2 * DEPTH), BF16),
            pltpu.VMEM((NY * NZ, ROWS, DEPTH), BF16),
            pltpu.VMEM((NY * NZ, ROWS, DEPTH), BF16),
            pltpu.VMEM((GROUPS, ROWS, DEPTH), BF16),
            pltpu.VMEM((2, DEPTH, DOC), BF16),
            pltpu.VMEM((DEPTH, NZ * SYS_Y), BF16),
            pltpu.VMEM((NY * NZ, DEPTH, ROWS), BF16),
            pltpu.VMEM((NY * NZ, 1, ROWS), F32),
            pltpu.VMEM((NY * NZ, DEPTH, ROWS), BF16),
            pltpu.VMEM((NY * NZ, 1, ROWS), F32),
            pltpu.VMEM((GROUPS, DEPTH, ROWS), F32),
            pltpu.VMEM((GROUPS, 1, ROWS), F32),
            pltpu.VMEM((GROUPS, 1, ROWS), F32),
            pltpu.VMEM((REQ, SUF, HEADS * DEPTH), BF16),
            pltpu.VMEM((REQ, SUF, HEADS * DEPTH), BF16),
            pltpu.VMEM((DOC, ROWS), F32),
            pltpu.VMEM((DOC, ROWS), F32),
            pltpu.VMEM((NY, DEPTH, ROWS), F32),
            pltpu.VMEM((NY, 1, ROWS), F32),
            pltpu.VMEM((NY, 1, ROWS), F32),
            dma((5,)),
            dma((2, 4, PARTS)), dma((2, 4, PARTS)),
            dma((2, 4)), dma((2, 4)),
            dma((3,)), dma((3,)),
            dma((3, stages)), dma((3, stages)),
            dma((3, stages)), dma((3, stages)),
            dma((3, stages)), dma((3, stages)),
            dma((7,)), dma((7,)),
        ],
        compiler_params=pltpu.CompilerParams(
            collective_id=0, has_side_effects=True, vmem_limit_bytes=56 << 20
        ),
        name="cascade",
    )(
        plan,
        suffix_len,
        queries,
        suffix_kv.reshape(REQ, SUF, 2 * DEPTH),
        sys_kv.reshape(32, 2 * DEPTH),
        doc_kv.reshape(1, DOC, 2 * DEPTH),
        conv_kv.reshape(GROUPS, CONV, 2 * DEPTH),
    )


def solution(mesh):
    placed = (
        P("kv", None, "tp"),
        P("kv", None, "tp", None),
        P("kv"),
        P("kv", "tp", None),
        P("kv", None, "tp", None),
        P(),
        P("kv"),
        P("kv", None, "tp", None),
        P("kv"),
    )
    return jax.shard_map(
        on_device,
        mesh=mesh,
        in_specs=placed,
        out_specs=P(("kv", "tp"), None, None),
        check_vma=False,
    )
```

```python
import functools
import math

import jax
import jax.numpy as jnp
from jax import lax
from jax.experimental import pallas as pl
from jax.experimental.pallas import tpu as pltpu
from jax.sharding import PartitionSpec as P

MESH = pl.DeviceIdType.MESH
F32 = jnp.float32
BF16 = jnp.bfloat16

NY, NZ, NT = 4, 8, 8
REQ, SUF, HEADS, DEPTH = 32, 16, 8, 128
GROUPS = REQ // 2
ROWS = 2 * SUF * HEADS
DOC, CONV, SYS_Y = 1024, 256, 128
HALF = DOC // 2
PARTS = 4
PIECE = DOC // PARTS
LOG2E = math.log2(math.e)
SCALE2 = LOG2E / math.sqrt(DEPTH)

SLOT_A, SLOT_B, GRP_A, GRP_B, GRP_SLOT, REQ_AT = range(6)

STAGES = ((0, 1), (1, 2), (3, 2), (5, 2), (7, 1))
PLACE_REL = (0, 1, 7, 2, 6, 3, 5, 4)
REL_PLACE = (0, 1, 3, 5, 7, 6, 4, 2)
SYS_FIRST = 5 * SYS_Y


def make_plan(homes, docs_of, convs, y, z):
    shape = (REQ, 128)
    sub = lax.broadcasted_iota(jnp.int32, shape, 0)
    lane = lax.broadcasted_iota(jnp.int32, shape, 1)

    def wide(row):
        return jnp.concatenate([jnp.broadcast_to(row, (REQ, REQ))] * (128 // REQ), axis=1)

    def column(row):
        return jnp.sum(jnp.where(sub == lane, wide(row), 0), axis=1, keepdims=True)

    doc = column(docs_of)
    group = column(convs) & (GROUPS - 1)
    holder = jnp.sum(jnp.where(doc == lane, wide(homes), 0), axis=1, keepdims=True)
    dy = ((holder >> 3) - y) & (NY - 1)
    rel = (holder - z) & (NZ - 1)
    place = jnp.where(rel == 0, 0, jnp.where(rel <= NZ // 2, 2 * rel - 1, 2 * (NZ - rel)))
    slot = dy * NZ + place
    in_slot = slot == lane
    in_group = group == lane
    earlier = (group == (wide(convs) & (GROUPS - 1))) & (sub < lane)

    def high(mask, value):
        return jnp.max(jnp.where(mask, value, 0), axis=0, keepdims=True)

    def low(mask):
        return high(mask, REQ - sub) * -1 + REQ * high(mask, 1 + 0 * sub)

    seen = high(earlier, 1 + 0 * sub)
    own = wide(convs)[:1] & (GROUPS - 1)
    return [low(in_slot), high(in_slot, sub), low(in_group), high(in_group, sub), high(in_group, slot), own * 2 + seen]


def scores(keys, rows):
    return lax.dot_general(keys, rows, (((1,), (1,)), ((), ())), preferred_element_type=F32)


def mix(values, weights):
    return lax.dot_general(values, weights, (((0,), (0,)), ((), ())), preferred_element_type=F32)


def mix_t(values_t, weights):
    return lax.dot_general(values_t, weights, (((1,), (0,)), ((), ())), preferred_element_type=F32)


def main_kernel(
    homes, docs_of, convs, lens, q_hbm, suf_hbm, sys_hbm, doc_hbm, conv_hbm, out_hbm,
    q_ref, suf_ref, conv_ref, docs, sysb, qs, qin, gq, vt, sysvt, ret_o, ret_l, d_o, d_l,
    l_acc, l_m, l_t, res, outst, s_a, s_b, p_acc, p_m, p_t, plan_v, plan,
    in_sem, doc_ss, doc_rs, sys_ss, sys_rs, sysy_ss, sysy_rs, q_ss, q_rs, o_ss, o_rs, e_ss, e_rs,
    x_ss, x_rs,
):
    kv, tp = lax.axis_index("kv"), lax.axis_index("tp")
    y, z = kv // NZ, kv % NZ
    z_right = y * NZ + lax.rem(z + 1, NZ)
    z_left = y * NZ + lax.rem(z + NZ - 1, NZ)

    def y_peer(k):
        return lax.rem(y + k, NY) * NZ + z

    def t_peer(k):
        return lax.rem(tp + k, NT)

    barrier = pltpu.get_barrier_semaphore()
    peers = [(z_right, tp), (z_left, tp)]
    peers += [(y_peer(k), tp) for k in range(1, NY)]
    peers += [(kv, t_peer(k)) for k in range(1, NT)]
    loads = [
        pltpu.make_async_copy(q_hbm, q_ref, in_sem.at[0]),
        pltpu.make_async_copy(sys_hbm, sysb.at[pl.ds(0, 32)], in_sem.at[1]),
        pltpu.make_async_copy(doc_hbm.at[0], docs.at[0], in_sem.at[2]),
        pltpu.make_async_copy(suf_hbm, suf_ref, in_sem.at[3]),
        pltpu.make_async_copy(conv_hbm, conv_ref, in_sem.at[4]),
    ]
    for load in loads:
        load.start()
    for peer in peers:
        pl.semaphore_signal(barrier, inc=1, device_id=peer, device_id_type=MESH)
    pl.semaphore_wait(barrier, len(peers))

    def remote(src, dst, ss, rs, peer):
        return pltpu.make_async_remote_copy(
            src_ref=src, dst_ref=dst, send_sem=ss, recv_sem=rs, device_id=peer, device_id_type=MESH
        )

    def doc_copy(way, hop, part):
        rel_src = (NZ - (hop - 1)) % NZ if way == 0 else hop - 1
        rel_dst = NZ - hop if way == 0 else hop
        rows = pl.ds(part * PIECE, PIECE)
        src = doc_hbm.at[0, rows] if hop == 1 else docs.at[rel_src, rows]
        peer = (z_right if way == 0 else z_left, tp)
        return remote(
            src, docs.at[rel_dst, rows], doc_ss.at[way, hop - 1, part], doc_rs.at[way, hop - 1, part], peer
        )

    def sys_copy(way, hop):
        rel_src = (NZ - (hop - 1)) % NZ if way == 0 else hop - 1
        rel_dst = NZ - hop if way == 0 else hop
        at, size = (0, SYS_Y) if hop < 4 else (way * SYS_Y // 2, SYS_Y // 2)
        peer = (z_right if way == 0 else z_left, tp)
        return remote(
            sysb.at[pl.ds(REL_PLACE[rel_src] * SYS_Y + at, size)],
            sysb.at[pl.ds(REL_PLACE[rel_dst] * SYS_Y + at, size)],
            sys_ss.at[way, hop - 1], sys_rs.at[way, hop - 1], peer,
        )

    def sys_y_copy(k):
        return remote(
            sys_hbm, sysb.at[pl.ds(32 * (NY - k), 32)], sysy_ss.at[k - 1], sysy_rs.at[k - 1],
            (y_peer(k), tp),
        )

    def q_copy(k, stage):
        first, count = STAGES[stage]
        return remote(
            qs.at[pl.ds(k * NZ + first, count)], qin.at[pl.ds((NY - k) * NZ + first, count)],
            q_ss.at[k - 1, stage], q_rs.at[k - 1, stage], (y_peer(k), tp),
        )

    def o_copy(k, stage):
        first, count = STAGES[stage]
        return remote(
            ret_o.at[pl.ds(k * NZ + first, count)], d_o.at[pl.ds((NY - k) * NZ + first, count)],
            o_ss.at[k - 1, stage], o_rs.at[k - 1, stage], (y_peer(k), tp),
        )

    def e_copy(k, stage):
        first, count = STAGES[stage]
        return remote(
            ret_l.at[pl.ds(k * NZ + first, count)], d_l.at[pl.ds((NY - k) * NZ + first, count)],
            e_ss.at[k - 1, stage], e_rs.at[k - 1, stage], (y_peer(k), tp),
        )

    sent = []

    def start(copy):
        copy.start()
        sent.append(copy)

    def doc_hop(hop, part):
        for way in range(2):
            if hop == 4 and way != part // 2:
                continue
            doc_copy(way, hop, part).wait_recv()
            if hop < 3 or (hop == 3 and way == part // 2):
                start(doc_copy(way, hop + 1, part))

    def sys_take(hop):
        for way in range(2):
            sys_copy(way, hop).wait_recv()

    def sys_pass(hop):
        for way in range(2):
            start(sys_copy(way, hop + 1))

    for way in range(2):
        start(doc_copy(way, 1, 0))
    for k in (1, 3, 2):
        start(sys_y_copy(k))

    rows = make_plan(homes[...], docs_of[...], convs[...], y, z)
    plan_v[...] = jnp.concatenate(rows + [jnp.zeros((8 - len(rows), 128), jnp.int32)], axis=0)
    to_scalars = pltpu.make_async_copy(plan_v, plan, in_sem.at[5])
    to_scalars.start()

    loads[0].wait()
    to_scalars.wait()

    def tile_rows(a, b):
        parts = []
        for h in range(HEADS):
            lanes = slice(h * DEPTH, (h + 1) * DEPTH)
            parts += [a[:, lanes], b[:, lanes]]
        return jnp.concatenate(parts, axis=0)

    def fill_own(s, carry):
        qin[s] = tile_rows(q_ref[plan[SLOT_A, s]], q_ref[plan[SLOT_B, s]])
        return carry

    def fill_group(g, carry):
        gq[g] = tile_rows(q_ref[plan[GRP_A, g]], q_ref[plan[GRP_B, g]])
        return carry

    for stage, (first, count) in enumerate(STAGES):

        def fill_out(i, carry, first=first, count=count):
            s = (1 + i // count) * NZ + first + i % count
            qs[s] = tile_rows(q_ref[plan[SLOT_A, s]], q_ref[plan[SLOT_B, s]])
            return carry

        lax.fori_loop(0, (NY - 1) * count, fill_out, 0)
        for k in (1, 3, 2):
            start(q_copy(k, stage))
    loads[1].wait()
    for k in range(1, NY):
        sys_y_copy(k).wait_recv()
    for way in range(2):
        start(sys_copy(way, 1))
    for part in range(1, PARTS):
        for way in range(2):
            start(doc_copy(way, 1, part))
    lax.fori_loop(0, NZ, fill_own, 0)
    lax.fori_loop(0, GROUPS, fill_group, 0)

    def attend(n, parts, done):
        def score(u, buf, part, top):
            first, size, score_of, _ = part
            s = score_of(u)
            buf[first : first + size] = s
            high = jnp.max(s.reshape(size // 8, 8, ROWS), axis=0)
            return high if top is None else jnp.maximum(top, high)

        def weigh(u, buf, part, top, state):
            first, size, _, mix_of = part
            e = jnp.exp2(buf[first : first + size] * SCALE2 - top)
            total = jnp.sum(e.reshape(size // 8, 8, ROWS), axis=0)
            o = mix_of(u, e.astype(BF16))
            return (o, total) if state is None else (state[0] + o, state[1] + total)

        def both(u_next, buf_next, u, buf, top):
            high = state = None
            for part in parts:
                high = score(u_next, buf_next, part, high)
                state = weigh(u, buf, part, top, state)
            done(u, state[0], jnp.sum(state[1], axis=0, keepdims=True), top)
            return jnp.max(high, axis=0, keepdims=True) * SCALE2

        def pair(i, top):
            top = both(2 * i + 1, s_b, 2 * i, s_a, top)
            return both(lax.rem(2 * i + 2, n), s_a, 2 * i + 1, s_b, top)

        high = None
        for part in parts:
            high = score(0, s_a, part, high)
        lax.fori_loop(0, n // 2, pair, jnp.max(high, axis=0, keepdims=True) * SCALE2)

    def doc_stage(stage):
        first, count = STAGES[stage]
        rel = PLACE_REL[first]
        for k in (1, 3, 2):
            q_copy(NY - k, stage).wait_recv()
        for j in range(count):
            vt[j] = docs[PLACE_REL[first + j], :, DEPTH:].T

        def place_of(u):
            return source_of(u // count) * NZ + first + u % count

        def rel_of(u):
            return rel + (u % count) * (NZ - 2 * rel)

        def part(at):
            keys = pl.ds(at, HALF)
            return (
                at, HALF,
                lambda u: scores(docs[rel_of(u), keys, :DEPTH], qin[place_of(u)]),
                lambda u, e: mix_t(vt[u % count, :, at : at + HALF], e),
            )

        def done(u, acc, total, top):
            ret_o[place_of(u)] = (acc * (1.0 / total)).astype(BF16)
            ret_l[place_of(u)] = top + jnp.log(total) * LOG2E
            send_back(u, stage)

        attend(NY * count, [part(0), part(HALF)], done)
        keep_own(stage)

    def source_of(i):
        return lax.rem(i + 1, NY)

    def send_back(u, stage):
        count = STAGES[stage][1]
        k = source_of(u // count)

        @pl.when((u % count == count - 1) & (k > 0))
        def _():
            o_copy(k, stage).start()
            e_copy(k, stage).start()

    def keep_own(stage):
        first, count = STAGES[stage]
        for k in range(1, NY):
            sent.append(o_copy(k, stage))
            sent.append(e_copy(k, stage))
        for j in range(first, first + count):
            d_o[j] = ret_o[j]
            d_l[j] = ret_l[j]

    def last_stage():
        stage = len(STAGES) - 1
        first, rel = STAGES[stage][0], PLACE_REL[STAGES[stage][0]]
        for k in (1, 3, 2):
            q_copy(NY - k, stage).wait_recv()

        def part(at):
            keys = pl.ds(at, PIECE)
            return (
                at, PIECE,
                lambda u: scores(docs[rel, keys, :DEPTH], qin[source_of(u) * NZ + first]),
                lambda u, e: mix_t(vt[0, :, at : at + PIECE], e),
            )

        def hold(u, acc, total, top):
            p_m[u] = top
            p_t[u] = total
            p_acc[u] = acc

        def done(u, acc, total, top):
            high = jnp.maximum(p_m[u], top)
            w_old = jnp.exp2(p_m[u] - high)
            w_new = jnp.exp2(top - high)
            total = p_t[u] * w_old + total * w_new
            place = source_of(u) * NZ + first
            ret_o[place] = ((p_acc[u] * w_old + acc * w_new) * (1.0 / total)).astype(BF16)
            ret_l[place] = high + jnp.log(total) * LOG2E
            send_back(u, stage)

        for pieces, finish in (((0, 2), hold), ((1, 3), done)):
            for piece in pieces:
                at = piece * PIECE
                doc_hop(4, piece)
                vt[0, :, at : at + PIECE] = docs[rel, at : at + PIECE, DEPTH:].T
            attend(NY, [part(piece * PIECE) for piece in pieces], finish)
        keep_own(stage)

    loads[3].wait()
    loads[4].wait()
    key_at = lax.broadcasted_iota(jnp.int32, (2 * SUF, ROWS), 0)
    row_at = lax.broadcasted_iota(jnp.int32, (2 * SUF, ROWS), 1)
    readable = ((row_at // SUF) % 2 == key_at // SUF) & (key_at % SUF <= row_at % SUF)

    def own_tokens(g, lanes):
        return jnp.concatenate(
            [suf_ref[plan[GRP_A, g], :, lanes], suf_ref[plan[GRP_B, g], :, lanes]], axis=0
        )

    conv_parts = [
        (
            0, CONV,
            lambda g: scores(conv_ref[g, :, :DEPTH], gq[g]),
            lambda g, e: mix(conv_ref[g, :, DEPTH:], e),
        ),
        (
            CONV, 2 * SUF,
            lambda g: jnp.where(readable, scores(own_tokens(g, slice(0, DEPTH)), gq[g]), -1e30),
            lambda g, e: mix(own_tokens(g, slice(DEPTH, 2 * DEPTH)), e),
        ),
    ]

    def conv_done(g, acc, total, top):
        l_m[g] = top
        l_t[g] = total
        l_acc[g] = acc

    def sys_part(at, size):
        keys = pl.ds(at, size)
        return (
            at, size,
            lambda g: scores(sysb[keys, :DEPTH], gq[g]),
            lambda g, e: mix_t(sysvt[:, at : at + size], e),
        )

    def turn_sys(first, last):
        for place in range(first, last):
            at = place * SYS_Y
            sysvt[:, at : at + SYS_Y] = sysb[at : at + SYS_Y, DEPTH:].T

    def sys_done(g, acc, total, top):
        high = jnp.maximum(l_m[g], top)
        w_old = jnp.exp2(l_m[g] - high)
        w_new = jnp.exp2(top - high)
        l_m[g] = high
        l_t[g] = l_t[g] * w_old + total * w_new
        l_acc[g] = l_acc[g] * w_old + acc * w_new

    attend(GROUPS, conv_parts, conv_done)
    sys_take(1)
    sys_pass(1)
    doc_hop(1, 0)
    loads[2].wait()
    doc_stage(0)
    doc_hop(1, 1)
    doc_hop(1, 2)
    doc_hop(1, 3)
    doc_stage(1)
    sys_take(2)
    doc_hop(2, 0)
    turn_sys(0, 5)
    attend(GROUPS, [sys_part(0, 384), sys_part(384, SYS_FIRST - 384)], sys_done)
    doc_hop(2, 1)
    doc_hop(2, 2)
    doc_hop(2, 3)
    sys_pass(2)
    doc_stage(2)
    for part in range(PARTS):
        doc_hop(3, part)
    sys_take(3)
    sys_pass(3)
    doc_stage(3)
    last_stage()
    sys_take(4)
    turn_sys(5, 8)
    attend(GROUPS, [sys_part(SYS_FIRST, NZ * SYS_Y - SYS_FIRST)], sys_done)
    for stage in range(len(STAGES)):
        for k in range(1, NY):
            o_copy(k, stage).wait_recv()
            e_copy(k, stage).wait_recv()

    def join(g, carry):
        slot = plan[GRP_SLOT, g]
        lse = d_l[slot]
        top = jnp.maximum(lse, l_m[g])
        w_doc = jnp.exp2(lse - top)
        w_loc = jnp.exp2(l_m[g] - top)
        upper = w_doc * d_o[slot].astype(F32) + w_loc * l_acc[g]
        out = (upper / (w_doc + w_loc * l_t[g])).T.astype(BF16)
        for h in range(HEADS):
            for p in range(2):
                first = (h * 2 + p) * SUF
                res[g * 2 + p, :, h * DEPTH : (h + 1) * DEPTH] = out[first : first + SUF]
        return carry

    lax.fori_loop(0, GROUPS, join, 0)
    token = lax.broadcasted_iota(jnp.int32, (SUF, HEADS * DEPTH), 0)

    share = REQ // NT
    lanes = pl.ds(pl.multiple_of(tp * HEADS * DEPTH, 128), HEADS * DEPTH)

    def x_copy(k):
        return remote(
            outst.at[pl.ds(t_peer(k) * share, share)], out_hbm.at[:, :, lanes],
            x_ss.at[k - 1], x_rs.at[k - 1], (kv, t_peer(k)),
        )

    own = pltpu.make_async_copy(
        outst.at[pl.ds(tp * share, share)], out_hbm.at[:, :, lanes], in_sem.at[0]
    )
    for k in (4, 3, 5, 2, 6, 1, 7, 0):
        for i in range(share):
            r = t_peer(k) * share + i
            value = res[plan[REQ_AT, r]]
            outst[r] = jnp.where(token < lens[r], value, jnp.zeros_like(value))
        if k:
            start(x_copy(k))
        else:
            own.start()
    for copy in sent:
        copy.wait_send()
    own.wait()
    for k in range(1, NT):
        x_copy(k).wait_recv()


def on_device(queries, suffix_kv, suffix_len, sys_kv, doc_kv, doc_home, doc_of, conv_kv, conv_of):
    smem = pl.BlockSpec(memory_space=pltpu.SMEM)
    vmem = pl.BlockSpec(memory_space=pltpu.VMEM)
    hbm = pl.BlockSpec(memory_space=pl.ANY)
    dma = pltpu.SemaphoreType.DMA
    stages = len(STAGES)
    return pl.pallas_call(
        main_kernel,
        out_shape=pltpu.VMEM((REQ // NT, SUF, NT * HEADS * DEPTH), BF16),
        in_specs=[vmem] * 3 + [smem] + [hbm] * 5,
        out_specs=pl.BlockSpec(memory_space=pltpu.VMEM),
        scratch_shapes=[
            pltpu.VMEM((REQ, SUF, HEADS * DEPTH), BF16),
            pltpu.VMEM((REQ, SUF, 2 * DEPTH), BF16),
            pltpu.VMEM((GROUPS, CONV, 2 * DEPTH), BF16),
            pltpu.VMEM((NZ, DOC, 2 * DEPTH), BF16),
            pltpu.VMEM((NZ * SYS_Y, 2 * DEPTH), BF16),
            pltpu.VMEM((NY * NZ, ROWS, DEPTH), BF16),
            pltpu.VMEM((NY * NZ, ROWS, DEPTH), BF16),
            pltpu.VMEM((GROUPS, ROWS, DEPTH), BF16),
            pltpu.VMEM((2, DEPTH, DOC), BF16),
            pltpu.VMEM((DEPTH, NZ * SYS_Y), BF16),
            pltpu.VMEM((NY * NZ, DEPTH, ROWS), BF16),
            pltpu.VMEM((NY * NZ, 1, ROWS), F32),
            pltpu.VMEM((NY * NZ, DEPTH, ROWS), BF16),
            pltpu.VMEM((NY * NZ, 1, ROWS), F32),
            pltpu.VMEM((GROUPS, DEPTH, ROWS), F32),
            pltpu.VMEM((GROUPS, 1, ROWS), F32),
            pltpu.VMEM((GROUPS, 1, ROWS), F32),
            pltpu.VMEM((REQ, SUF, HEADS * DEPTH), BF16),
            pltpu.VMEM((REQ, SUF, HEADS * DEPTH), BF16),
            pltpu.VMEM((DOC, ROWS), F32),
            pltpu.VMEM((DOC, ROWS), F32),
            pltpu.VMEM((NY, DEPTH, ROWS), F32),
            pltpu.VMEM((NY, 1, ROWS), F32),
            pltpu.VMEM((NY, 1, ROWS), F32),
            pltpu.VMEM((8, 128), jnp.int32),
            pltpu.SMEM((8, 128), jnp.int32),
            dma((6,)),
            dma((2, 4, PARTS)), dma((2, 4, PARTS)),
            dma((2, 4)), dma((2, 4)),
            dma((3,)), dma((3,)),
            dma((3, stages)), dma((3, stages)),
            dma((3, stages)), dma((3, stages)),
            dma((3, stages)), dma((3, stages)),
            dma((7,)), dma((7,)),
        ],
        compiler_params=pltpu.CompilerParams(
            collective_id=0, has_side_effects=True, vmem_limit_bytes=56 << 20
        ),
        name="cascade",
    )(
        doc_home.reshape(1, REQ),
        doc_of.reshape(1, REQ),
        conv_of.reshape(1, REQ),
        suffix_len,
        queries,
        suffix_kv.reshape(REQ, SUF, 2 * DEPTH),
        sys_kv.reshape(32, 2 * DEPTH),
        doc_kv.reshape(1, DOC, 2 * DEPTH),
        conv_kv.reshape(GROUPS, CONV, 2 * DEPTH),
    )


def solution(mesh):
    placed = (
        P("kv", None, "tp"),
        P("kv", None, "tp", None),
        P("kv"),
        P("kv", "tp", None),
        P("kv", None, "tp", None),
        P(),
        P("kv"),
        P("kv", None, "tp", None),
        P("kv"),
    )
    return jax.shard_map(
        on_device,
        mesh=mesh,
        in_specs=placed,
        out_specs=P(("kv", "tp"), None, None),
        check_vma=False,
    )
```

```python
import functools
import math

import jax
import jax.numpy as jnp
from jax import lax
from jax.experimental import pallas as pl
from jax.experimental.pallas import tpu as pltpu
from jax.sharding import PartitionSpec as P

MESH = pl.DeviceIdType.MESH
F32 = jnp.float32
BF16 = jnp.bfloat16

NY, NZ, NT = 4, 8, 8
REQ, SUF, HEADS, DEPTH = 32, 16, 8, 128
GROUPS = REQ // 2
ROWS = 2 * SUF * HEADS
DOC, CONV, SYS_Y = 1024, 256, 128
HALF = DOC // 2
PARTS = 4
PIECE = DOC // PARTS
LOG2E = math.log2(math.e)
SCALE2 = LOG2E / math.sqrt(DEPTH)

SLOT_A, SLOT_B, GRP_A, GRP_B, GRP_SLOT, REQ_AT = range(6)

STAGES = ((0, 1), (1, 2), (3, 2), (5, 2), (7, 1))
PLACE_REL = (0, 1, 7, 2, 6, 3, 5, 4)
REL_PLACE = (0, 1, 3, 5, 7, 6, 4, 2)
SYS_FIRST = 5 * SYS_Y


def make_plan(homes, docs_of, convs, y, z):
    shape = (REQ, 128)
    sub = lax.broadcasted_iota(jnp.int32, shape, 0)
    lane = lax.broadcasted_iota(jnp.int32, shape, 1)

    def wide(row):
        return jnp.concatenate([jnp.broadcast_to(row, (REQ, REQ))] * (128 // REQ), axis=1)

    def column(row):
        return jnp.sum(jnp.where(sub == lane, wide(row), 0), axis=1, keepdims=True)

    doc = column(docs_of)
    group = column(convs) & (GROUPS - 1)
    holder = jnp.sum(jnp.where(doc == lane, wide(homes), 0), axis=1, keepdims=True)
    dy = ((holder >> 3) - y) & (NY - 1)
    rel = (holder - z) & (NZ - 1)
    place = jnp.where(rel == 0, 0, jnp.where(rel <= NZ // 2, 2 * rel - 1, 2 * (NZ - rel)))
    slot = dy * NZ + place
    in_slot = slot == lane
    in_group = group == lane
    earlier = (group == (wide(convs) & (GROUPS - 1))) & (sub < lane)

    def high(mask, value):
        return jnp.max(jnp.where(mask, value, 0), axis=0, keepdims=True)

    def low(mask):
        return high(mask, REQ - sub) * -1 + REQ * high(mask, 1 + 0 * sub)

    seen = high(earlier, 1 + 0 * sub)
    own = wide(convs)[:1] & (GROUPS - 1)
    return [low(in_slot), high(in_slot, sub), low(in_group), high(in_group, sub), high(in_group, slot), own * 2 + seen]


def scores(keys, rows):
    return lax.dot_general(keys, rows, (((1,), (1,)), ((), ())), preferred_element_type=F32)


def mix(values, weights):
    return lax.dot_general(values, weights, (((0,), (0,)), ((), ())), preferred_element_type=F32)


def mix_t(values_t, weights):
    return lax.dot_general(values_t, weights, (((1,), (0,)), ((), ())), preferred_element_type=F32)


def main_kernel(
    homes, docs_of, convs, lens, q_hbm, suf_hbm, sys_hbm, doc_hbm, conv_hbm, out_hbm,
    q_ref, suf_ref, conv_ref, docs, sysb, qs, qin, gq, vt, sysvt, ret_o, ret_l, d_o, d_l,
    l_acc, l_m, l_t, outst, s_a, s_b, p_acc, p_m, p_t, plan_v, plan,
    in_sem, doc_ss, doc_rs, sys_ss, sys_rs, sysy_ss, sysy_rs, q_ss, q_rs, o_ss, o_rs, e_ss, e_rs,
    x_ss, x_rs,
):
    kv, tp = lax.axis_index("kv"), lax.axis_index("tp")
    y, z = kv // NZ, kv % NZ
    z_right = y * NZ + lax.rem(z + 1, NZ)
    z_left = y * NZ + lax.rem(z + NZ - 1, NZ)

    def y_peer(k):
        return lax.rem(y + k, NY) * NZ + z

    def t_peer(k):
        return lax.rem(tp + k, NT)

    barrier = pltpu.get_barrier_semaphore()
    peers = [(z_right, tp), (z_left, tp)]
    peers += [(y_peer(k), tp) for k in range(1, NY)]
    peers += [(kv, t_peer(k)) for k in range(1, NT)]
    loads = [
        pltpu.make_async_copy(q_hbm, q_ref, in_sem.at[0]),
        pltpu.make_async_copy(sys_hbm, sysb.at[pl.ds(0, 32)], in_sem.at[1]),
        pltpu.make_async_copy(doc_hbm.at[0], docs.at[0], in_sem.at[2]),
        pltpu.make_async_copy(suf_hbm, suf_ref, in_sem.at[3]),
        pltpu.make_async_copy(conv_hbm, conv_ref, in_sem.at[4]),
    ]
    for load in loads:
        load.start()
    for peer in peers:
        pl.semaphore_signal(barrier, inc=1, device_id=peer, device_id_type=MESH)
    pl.semaphore_wait(barrier, len(peers))

    def remote(src, dst, ss, rs, peer):
        return pltpu.make_async_remote_copy(
            src_ref=src, dst_ref=dst, send_sem=ss, recv_sem=rs, device_id=peer, device_id_type=MESH
        )

    def doc_copy(way, hop, part):
        rel_src = (NZ - (hop - 1)) % NZ if way == 0 else hop - 1
        rel_dst = NZ - hop if way == 0 else hop
        rows = pl.ds(part * PIECE, PIECE)
        src = doc_hbm.at[0, rows] if hop == 1 else docs.at[rel_src, rows]
        peer = (z_right if way == 0 else z_left, tp)
        return remote(
            src, docs.at[rel_dst, rows], doc_ss.at[way, hop - 1, part], doc_rs.at[way, hop - 1, part], peer
        )

    def sys_copy(way, hop):
        rel_src = (NZ - (hop - 1)) % NZ if way == 0 else hop - 1
        rel_dst = NZ - hop if way == 0 else hop
        at, size = (0, SYS_Y) if hop < 4 else (way * SYS_Y // 2, SYS_Y // 2)
        peer = (z_right if way == 0 else z_left, tp)
        return remote(
            sysb.at[pl.ds(REL_PLACE[rel_src] * SYS_Y + at, size)],
            sysb.at[pl.ds(REL_PLACE[rel_dst] * SYS_Y + at, size)],
            sys_ss.at[way, hop - 1], sys_rs.at[way, hop - 1], peer,
        )

    def sys_y_copy(k):
        return remote(
            sys_hbm, sysb.at[pl.ds(32 * (NY - k), 32)], sysy_ss.at[k - 1], sysy_rs.at[k - 1],
            (y_peer(k), tp),
        )

    def q_copy(k, stage):
        first, count = STAGES[stage]
        return remote(
            qs.at[pl.ds(k * NZ + first, count)], qin.at[pl.ds((NY - k) * NZ + first, count)],
            q_ss.at[k - 1, stage], q_rs.at[k - 1, stage], (y_peer(k), tp),
        )

    def o_copy(k, stage):
        first, count = STAGES[stage]
        return remote(
            ret_o.at[pl.ds(k * NZ + first, count)], d_o.at[pl.ds((NY - k) * NZ + first, count)],
            o_ss.at[k - 1, stage], o_rs.at[k - 1, stage], (y_peer(k), tp),
        )

    def e_copy(k, stage):
        first, count = STAGES[stage]
        return remote(
            ret_l.at[pl.ds(k * NZ + first, count)], d_l.at[pl.ds((NY - k) * NZ + first, count)],
            e_ss.at[k - 1, stage], e_rs.at[k - 1, stage], (y_peer(k), tp),
        )

    sent = []

    def start(copy):
        copy.start()
        sent.append(copy)

    def doc_hop(hop, part):
        for way in range(2):
            if hop == 4 and way != part // 2:
                continue
            doc_copy(way, hop, part).wait_recv()
            if hop < 3 or (hop == 3 and way == part // 2):
                start(doc_copy(way, hop + 1, part))

    def sys_take(hop):
        for way in range(2):
            sys_copy(way, hop).wait_recv()

    def sys_pass(hop):
        for way in range(2):
            start(sys_copy(way, hop + 1))

    for way in range(2):
        start(doc_copy(way, 1, 0))
    for k in (1, 3, 2):
        start(sys_y_copy(k))

    rows = make_plan(homes[...], docs_of[...], convs[...], y, z)
    plan_v[...] = jnp.concatenate(rows + [jnp.zeros((8 - len(rows), 128), jnp.int32)], axis=0)
    to_scalars = pltpu.make_async_copy(plan_v, plan, in_sem.at[5])
    to_scalars.start()

    loads[0].wait()
    to_scalars.wait()

    def tile_rows(a, b):
        parts = []
        for rows in (a, b):
            parts += [rows[:, h * DEPTH : (h + 1) * DEPTH] for h in range(HEADS)]
        return jnp.concatenate(parts, axis=0)

    def fill_own(s, carry):
        qin[s] = tile_rows(q_ref[plan[SLOT_A, s]], q_ref[plan[SLOT_B, s]])
        return carry

    def fill_group(g, carry):
        gq[g] = tile_rows(q_ref[plan[GRP_A, g]], q_ref[plan[GRP_B, g]])
        return carry

    for stage, (first, count) in enumerate(STAGES):

        def fill_out(i, carry, first=first, count=count):
            s = (1 + i // count) * NZ + first + i % count
            qs[s] = tile_rows(q_ref[plan[SLOT_A, s]], q_ref[plan[SLOT_B, s]])
            return carry

        lax.fori_loop(0, (NY - 1) * count, fill_out, 0)
        for k in (1, 3, 2):
            start(q_copy(k, stage))
    loads[1].wait()
    for k in range(1, NY):
        sys_y_copy(k).wait_recv()
    for way in range(2):
        start(sys_copy(way, 1))
    for part in range(1, PARTS):
        for way in range(2):
            start(doc_copy(way, 1, part))
    lax.fori_loop(0, NZ, fill_own, 0)
    lax.fori_loop(0, GROUPS, fill_group, 0)

    def attend(n, parts, done):
        def score(u, buf, part, top):
            first, size, score_of, _ = part
            s = score_of(u)
            buf[first : first + size] = s
            high = jnp.max(s.reshape(size // 8, 8, ROWS), axis=0)
            return high if top is None else jnp.maximum(top, high)

        def weigh(u, buf, part, top, state):
            first, size, _, mix_of = part
            e = jnp.exp2(buf[first : first + size] * SCALE2 - top)
            total = jnp.sum(e.reshape(size // 8, 8, ROWS), axis=0)
            o = mix_of(u, e.astype(BF16))
            return (o, total) if state is None else (state[0] + o, state[1] + total)

        def both(u_next, buf_next, u, buf, top):
            high = state = None
            for part in parts:
                high = score(u_next, buf_next, part, high)
                state = weigh(u, buf, part, top, state)
            done(u, state[0], jnp.sum(state[1], axis=0, keepdims=True), top)
            return jnp.max(high, axis=0, keepdims=True) * SCALE2

        def pair(i, top):
            top = both(2 * i + 1, s_b, 2 * i, s_a, top)
            return both(lax.rem(2 * i + 2, n), s_a, 2 * i + 1, s_b, top)

        high = None
        for part in parts:
            high = score(0, s_a, part, high)
        lax.fori_loop(0, n // 2, pair, jnp.max(high, axis=0, keepdims=True) * SCALE2)

    def doc_stage(stage):
        first, count = STAGES[stage]
        rel = PLACE_REL[first]
        for k in (1, 3, 2):
            q_copy(NY - k, stage).wait_recv()
        for j in range(count):
            vt[j] = docs[PLACE_REL[first + j], :, DEPTH:].T

        def place_of(u):
            return source_of(u // count) * NZ + first + u % count

        def rel_of(u):
            return rel + (u % count) * (NZ - 2 * rel)

        def part(at):
            keys = pl.ds(at, HALF)
            return (
                at, HALF,
                lambda u: scores(docs[rel_of(u), keys, :DEPTH], qin[place_of(u)]),
                lambda u, e: mix_t(vt[u % count, :, at : at + HALF], e),
            )

        def done(u, acc, total, top):
            ret_o[place_of(u)] = (acc * (1.0 / total)).astype(BF16)
            ret_l[place_of(u)] = top + jnp.log(total) * LOG2E
            send_back(u, stage)

        attend(NY * count, [part(0), part(HALF)], done)
        keep_own(stage)

    def source_of(i):
        return lax.rem(i + 1, NY)

    def send_back(u, stage):
        count = STAGES[stage][1]
        k = source_of(u // count)

        @pl.when((u % count == count - 1) & (k > 0))
        def _():
            o_copy(k, stage).start()
            e_copy(k, stage).start()

    def keep_own(stage):
        first, count = STAGES[stage]
        for k in range(1, NY):
            sent.append(o_copy(k, stage))
            sent.append(e_copy(k, stage))
        for j in range(first, first + count):
            d_o[j] = ret_o[j]
            d_l[j] = ret_l[j]

    def last_stage():
        stage = len(STAGES) - 1
        first, rel = STAGES[stage][0], PLACE_REL[STAGES[stage][0]]
        for k in (1, 3, 2):
            q_copy(NY - k, stage).wait_recv()

        def part(at):
            keys = pl.ds(at, PIECE)
            return (
                at, PIECE,
                lambda u: scores(docs[rel, keys, :DEPTH], qin[source_of(u) * NZ + first]),
                lambda u, e: mix_t(vt[0, :, at : at + PIECE], e),
            )

        def hold(u, acc, total, top):
            p_m[u] = top
            p_t[u] = total
            p_acc[u] = acc

        def done(u, acc, total, top):
            high = jnp.maximum(p_m[u], top)
            w_old = jnp.exp2(p_m[u] - high)
            w_new = jnp.exp2(top - high)
            total = p_t[u] * w_old + total * w_new
            place = source_of(u) * NZ + first
            ret_o[place] = ((p_acc[u] * w_old + acc * w_new) * (1.0 / total)).astype(BF16)
            ret_l[place] = high + jnp.log(total) * LOG2E
            send_back(u, stage)

        for pieces, finish in (((0, 2), hold), ((1, 3), done)):
            for piece in pieces:
                at = piece * PIECE
                doc_hop(4, piece)
                vt[0, :, at : at + PIECE] = docs[rel, at : at + PIECE, DEPTH:].T
            attend(NY, [part(piece * PIECE) for piece in pieces], finish)
        keep_own(stage)

    loads[3].wait()
    loads[4].wait()
    key_at = lax.broadcasted_iota(jnp.int32, (2 * SUF, ROWS), 0)
    row_at = lax.broadcasted_iota(jnp.int32, (2 * SUF, ROWS), 1)
    readable = (row_at // (SUF * HEADS) == key_at // SUF) & (key_at % SUF <= row_at % SUF)

    def own_tokens(g, lanes):
        return jnp.concatenate(
            [suf_ref[plan[GRP_A, g], :, lanes], suf_ref[plan[GRP_B, g], :, lanes]], axis=0
        )

    conv_parts = [
        (
            0, CONV,
            lambda g: scores(conv_ref[g, :, :DEPTH], gq[g]),
            lambda g, e: mix(conv_ref[g, :, DEPTH:], e),
        ),
        (
            CONV, 2 * SUF,
            lambda g: jnp.where(readable, scores(own_tokens(g, slice(0, DEPTH)), gq[g]), -1e30),
            lambda g, e: mix(own_tokens(g, slice(DEPTH, 2 * DEPTH)), e),
        ),
    ]

    def conv_done(g, acc, total, top):
        l_m[g] = top
        l_t[g] = total
        l_acc[g] = acc

    def sys_part(at, size):
        keys = pl.ds(at, size)
        return (
            at, size,
            lambda g: scores(sysb[keys, :DEPTH], gq[g]),
            lambda g, e: mix_t(sysvt[:, at : at + size], e),
        )

    def turn_sys(first, last):
        for place in range(first, last):
            at = place * SYS_Y
            sysvt[:, at : at + SYS_Y] = sysb[at : at + SYS_Y, DEPTH:].T

    def sys_done(g, acc, total, top):
        high = jnp.maximum(l_m[g], top)
        w_old = jnp.exp2(l_m[g] - high)
        w_new = jnp.exp2(top - high)
        l_m[g] = high
        l_t[g] = l_t[g] * w_old + total * w_new
        l_acc[g] = l_acc[g] * w_old + acc * w_new

    attend(GROUPS, conv_parts, conv_done)
    sys_take(1)
    sys_pass(1)
    doc_hop(1, 0)
    loads[2].wait()
    doc_stage(0)
    doc_hop(1, 1)
    doc_hop(1, 2)
    doc_hop(1, 3)
    doc_stage(1)
    sys_take(2)
    doc_hop(2, 0)
    turn_sys(0, 5)
    attend(GROUPS, [sys_part(0, 384), sys_part(384, SYS_FIRST - 384)], sys_done)
    doc_hop(2, 1)
    doc_hop(2, 2)
    doc_hop(2, 3)
    sys_pass(2)
    doc_stage(2)
    for part in range(PARTS):
        doc_hop(3, part)
    sys_take(3)
    sys_pass(3)
    doc_stage(3)
    last_stage()
    sys_take(4)
    turn_sys(5, 8)
    attend(GROUPS, [sys_part(SYS_FIRST, NZ * SYS_Y - SYS_FIRST)], sys_done)
    for stage in range(len(STAGES)):
        for k in range(1, NY):
            o_copy(k, stage).wait_recv()
            e_copy(k, stage).wait_recv()

    token = lax.broadcasted_iota(jnp.int32, (SUF, HEADS * DEPTH), 0)


    def join(r):
        at = plan[REQ_AT, r]
        g, second = at // 2, at % 2 == 1
        slot = plan[GRP_SLOT, g]

        def half(rows):
            return jnp.where(second, rows[:, ROWS // 2 :], rows[:, : ROWS // 2])

        lse, local, total = half(d_l[slot]), half(l_m[g]), half(l_t[g])
        top = jnp.maximum(lse, local)
        w_doc = jnp.exp2(lse - top)
        w_loc = jnp.exp2(local - top)
        upper = w_doc * half(d_o[slot]).astype(F32) + w_loc * half(l_acc[g])
        out = (upper / (w_doc + w_loc * total)).T.astype(BF16)
        rows = [out[h * SUF : (h + 1) * SUF] for h in range(HEADS)]
        value = jnp.concatenate(rows, axis=1)
        return jnp.where(token < lens[r], value, jnp.zeros_like(value))

    share = REQ // NT
    lanes = pl.ds(pl.multiple_of(tp * HEADS * DEPTH, 128), HEADS * DEPTH)

    def x_copy(k):
        return remote(
            outst.at[pl.ds(t_peer(k) * share, share)], out_hbm.at[:, :, lanes],
            x_ss.at[k - 1], x_rs.at[k - 1], (kv, t_peer(k)),
        )

    own = pltpu.make_async_copy(
        outst.at[pl.ds(tp * share, share)], out_hbm.at[:, :, lanes], in_sem.at[0]
    )
    for k in (4, 3, 5, 2, 6, 1, 7, 0):
        for i in range(share):
            r = t_peer(k) * share + i
            outst[r] = join(r)
        if k:
            start(x_copy(k))
        else:
            own.start()
    for copy in sent:
        copy.wait_send()
    own.wait()
    for k in range(1, NT):
        x_copy(k).wait_recv()


def on_device(queries, suffix_kv, suffix_len, sys_kv, doc_kv, doc_home, doc_of, conv_kv, conv_of):
    smem = pl.BlockSpec(memory_space=pltpu.SMEM)
    vmem = pl.BlockSpec(memory_space=pltpu.VMEM)
    hbm = pl.BlockSpec(memory_space=pl.ANY)
    dma = pltpu.SemaphoreType.DMA
    stages = len(STAGES)
    return pl.pallas_call(
        main_kernel,
        out_shape=pltpu.VMEM((REQ // NT, SUF, NT * HEADS * DEPTH), BF16),
        in_specs=[vmem] * 3 + [smem] + [hbm] * 5,
        out_specs=pl.BlockSpec(memory_space=pltpu.VMEM),
        scratch_shapes=[
            pltpu.VMEM((REQ, SUF, HEADS * DEPTH), BF16),
            pltpu.VMEM((REQ, SUF, 2 * DEPTH), BF16),
            pltpu.VMEM((GROUPS, CONV, 2 * DEPTH), BF16),
            pltpu.VMEM((NZ, DOC, 2 * DEPTH), BF16),
            pltpu.VMEM((NZ * SYS_Y, 2 * DEPTH), BF16),
            pltpu.VMEM((NY * NZ, ROWS, DEPTH), BF16),
            pltpu.VMEM((NY * NZ, ROWS, DEPTH), BF16),
            pltpu.VMEM((GROUPS, ROWS, DEPTH), BF16),
            pltpu.VMEM((2, DEPTH, DOC), BF16),
            pltpu.VMEM((DEPTH, NZ * SYS_Y), BF16),
            pltpu.VMEM((NY * NZ, DEPTH, ROWS), BF16),
            pltpu.VMEM((NY * NZ, 1, ROWS), F32),
            pltpu.VMEM((NY * NZ, DEPTH, ROWS), BF16),
            pltpu.VMEM((NY * NZ, 1, ROWS), F32),
            pltpu.VMEM((GROUPS, DEPTH, ROWS), F32),
            pltpu.VMEM((GROUPS, 1, ROWS), F32),
            pltpu.VMEM((GROUPS, 1, ROWS), F32),
            pltpu.VMEM((REQ, SUF, HEADS * DEPTH), BF16),
            pltpu.VMEM((DOC, ROWS), F32),
            pltpu.VMEM((DOC, ROWS), F32),
            pltpu.VMEM((NY, DEPTH, ROWS), F32),
            pltpu.VMEM((NY, 1, ROWS), F32),
            pltpu.VMEM((NY, 1, ROWS), F32),
            pltpu.VMEM((8, 128), jnp.int32),
            pltpu.SMEM((8, 128), jnp.int32),
            dma((6,)),
            dma((2, 4, PARTS)), dma((2, 4, PARTS)),
            dma((2, 4)), dma((2, 4)),
            dma((3,)), dma((3,)),
            dma((3, stages)), dma((3, stages)),
            dma((3, stages)), dma((3, stages)),
            dma((3, stages)), dma((3, stages)),
            dma((7,)), dma((7,)),
        ],
        compiler_params=pltpu.CompilerParams(
            collective_id=0, has_side_effects=True, vmem_limit_bytes=56 << 20
        ),
        name="cascade",
    )(
        doc_home.reshape(1, REQ),
        doc_of.reshape(1, REQ),
        conv_of.reshape(1, REQ),
        suffix_len,
        queries,
        suffix_kv.reshape(REQ, SUF, 2 * DEPTH),
        sys_kv.reshape(32, 2 * DEPTH),
        doc_kv.reshape(1, DOC, 2 * DEPTH),
        conv_kv.reshape(GROUPS, CONV, 2 * DEPTH),
    )


def solution(mesh):
    placed = (
        P("kv", None, "tp"),
        P("kv", None, "tp", None),
        P("kv"),
        P("kv", "tp", None),
        P("kv", None, "tp", None),
        P(),
        P("kv"),
        P("kv", None, "tp", None),
        P("kv"),
    )
    return jax.shard_map(
        on_device,
        mesh=mesh,
        in_specs=placed,
        out_specs=P(("kv", "tp"), None, None),
        check_vma=False,
    )
```

```python
import functools
import math

import jax
import jax.numpy as jnp
from jax import lax
from jax.experimental import pallas as pl
from jax.experimental.pallas import tpu as pltpu
from jax.sharding import PartitionSpec as P

MESH = pl.DeviceIdType.MESH
F32 = jnp.float32
BF16 = jnp.bfloat16

NY, NZ, NT = 4, 8, 8
REQ, SUF, HEADS, DEPTH = 32, 16, 8, 128
GROUPS = REQ // 2
ROWS = 2 * SUF * HEADS
DOC, CONV, SYS_Y = 1024, 256, 128
HALF = DOC // 2
PARTS = 4
PIECE = DOC // PARTS
LOG2E = math.log2(math.e)
SCALE2 = LOG2E / math.sqrt(DEPTH)

SLOT_A, SLOT_B, GRP_A, GRP_B, GRP_SLOT, REQ_AT = range(6)

STAGES = ((0, 1), (1, 2), (3, 2), (5, 2), (7, 1))
PLACE_REL = (0, 1, 7, 2, 6, 3, 5, 4)
REL_PLACE = (0, 1, 3, 5, 7, 6, 4, 2)
SYS_FIRST = 5 * SYS_Y


def make_plan(homes, docs_of, convs, y, z):
    shape = (REQ, 128)
    sub = lax.broadcasted_iota(jnp.int32, shape, 0)
    lane = lax.broadcasted_iota(jnp.int32, shape, 1)

    def wide(row):
        return jnp.concatenate([jnp.broadcast_to(row, (REQ, REQ))] * (128 // REQ), axis=1)

    def column(row):
        return jnp.sum(jnp.where(sub == lane, wide(row), 0), axis=1, keepdims=True)

    doc = column(docs_of)
    group = column(convs) & (GROUPS - 1)
    holder = jnp.sum(jnp.where(doc == lane, wide(homes), 0), axis=1, keepdims=True)
    dy = ((holder >> 3) - y) & (NY - 1)
    rel = (holder - z) & (NZ - 1)
    place = jnp.where(rel == 0, 0, jnp.where(rel <= NZ // 2, 2 * rel - 1, 2 * (NZ - rel)))
    slot = dy * NZ + place
    in_slot = slot == lane
    in_group = group == lane
    earlier = (group == (wide(convs) & (GROUPS - 1))) & (sub < lane)

    def high(mask, value):
        return jnp.max(jnp.where(mask, value, 0), axis=0, keepdims=True)

    def low(mask):
        return high(mask, REQ - sub) * -1 + REQ * high(mask, 1 + 0 * sub)

    seen = high(earlier, 1 + 0 * sub)
    own = wide(convs)[:1] & (GROUPS - 1)
    return [low(in_slot), high(in_slot, sub), low(in_group), high(in_group, sub), high(in_group, slot), own * 2 + seen]


def scores(keys, rows):
    return lax.dot_general(keys, rows, (((1,), (1,)), ((), ())), preferred_element_type=F32)


def mix(values, weights):
    return lax.dot_general(values, weights, (((0,), (0,)), ((), ())), preferred_element_type=F32)


def mix_t(values_t, weights):
    return lax.dot_general(values_t, weights, (((1,), (0,)), ((), ())), preferred_element_type=F32)


def main_kernel(
    homes, docs_of, convs, lens, q_hbm, suf_hbm, sys_hbm, doc_hbm, conv_hbm, out_hbm,
    q_ref, suf_ref, conv_ref, docs, sysb, qs, qin, gq, vt, sysvt, ret_o, ret_l, d_o, d_l,
    l_acc, l_m, l_t, outst, s_a, s_b, p_acc, p_m, p_t, plan_v, plan,
    in_sem, doc_ss, doc_rs, sys_ss, sys_rs, sysy_ss, sysy_rs, q_ss, q_rs, o_ss, o_rs, e_ss, e_rs,
    x_ss, x_rs,
):
    kv, tp = lax.axis_index("kv"), lax.axis_index("tp")
    y, z = kv // NZ, kv % NZ
    z_right = y * NZ + lax.rem(z + 1, NZ)
    z_left = y * NZ + lax.rem(z + NZ - 1, NZ)

    def y_peer(k):
        return lax.rem(y + k, NY) * NZ + z

    def t_peer(k):
        return lax.rem(tp + k, NT)

    barrier = pltpu.get_barrier_semaphore()
    peers = [(z_right, tp), (z_left, tp)]
    peers += [(y_peer(k), tp) for k in range(1, NY)]
    peers += [(kv, t_peer(k)) for k in range(1, NT)]
    loads = [
        pltpu.make_async_copy(q_hbm, q_ref, in_sem.at[0]),
        pltpu.make_async_copy(sys_hbm, sysb.at[pl.ds(0, 32)], in_sem.at[1]),
        pltpu.make_async_copy(doc_hbm.at[0], docs.at[0], in_sem.at[2]),
        pltpu.make_async_copy(suf_hbm, suf_ref, in_sem.at[3]),
        pltpu.make_async_copy(conv_hbm, conv_ref, in_sem.at[4]),
    ]
    for load in loads:
        load.start()
    for peer in peers:
        pl.semaphore_signal(barrier, inc=1, device_id=peer, device_id_type=MESH)
    pl.semaphore_wait(barrier, len(peers))

    def remote(src, dst, ss, rs, peer):
        return pltpu.make_async_remote_copy(
            src_ref=src, dst_ref=dst, send_sem=ss, recv_sem=rs, device_id=peer, device_id_type=MESH
        )

    def doc_copy(way, hop, part):
        rel_src = (NZ - (hop - 1)) % NZ if way == 0 else hop - 1
        rel_dst = NZ - hop if way == 0 else hop
        rows = pl.ds(part * PIECE, PIECE)
        src = doc_hbm.at[0, rows] if hop == 1 else docs.at[rel_src, rows]
        peer = (z_right if way == 0 else z_left, tp)
        return remote(
            src, docs.at[rel_dst, rows], doc_ss.at[way, hop - 1, part], doc_rs.at[way, hop - 1, part], peer
        )

    def sys_copy(way, hop):
        rel_src = (NZ - (hop - 1)) % NZ if way == 0 else hop - 1
        rel_dst = NZ - hop if way == 0 else hop
        at, size = (0, SYS_Y) if hop < 4 else (way * SYS_Y // 2, SYS_Y // 2)
        peer = (z_right if way == 0 else z_left, tp)
        return remote(
            sysb.at[pl.ds(REL_PLACE[rel_src] * SYS_Y + at, size)],
            sysb.at[pl.ds(REL_PLACE[rel_dst] * SYS_Y + at, size)],
            sys_ss.at[way, hop - 1], sys_rs.at[way, hop - 1], peer,
        )

    def sys_y_copy(k):
        return remote(
            sys_hbm, sysb.at[pl.ds(32 * (NY - k), 32)], sysy_ss.at[k - 1], sysy_rs.at[k - 1],
            (y_peer(k), tp),
        )

    def q_copy(k, stage):
        first, count = STAGES[stage]
        return remote(
            qs.at[pl.ds(k * NZ + first, count)], qin.at[pl.ds((NY - k) * NZ + first, count)],
            q_ss.at[k - 1, stage], q_rs.at[k - 1, stage], (y_peer(k), tp),
        )

    def o_copy(k, stage):
        first, count = STAGES[stage]
        return remote(
            ret_o.at[pl.ds(k * NZ + first, count)], d_o.at[pl.ds((NY - k) * NZ + first, count)],
            o_ss.at[k - 1, stage], o_rs.at[k - 1, stage], (y_peer(k), tp),
        )

    def e_copy(k, stage):
        first, count = STAGES[stage]
        return remote(
            ret_l.at[pl.ds(k * NZ + first, count)], d_l.at[pl.ds((NY - k) * NZ + first, count)],
            e_ss.at[k - 1, stage], e_rs.at[k - 1, stage], (y_peer(k), tp),
        )

    sent = []

    def start(copy):
        copy.start()
        sent.append(copy)

    def doc_hop(hop, part):
        for way in range(2):
            if hop == 4 and way != part // 2:
                continue
            doc_copy(way, hop, part).wait_recv()
            if hop < 3 or (hop == 3 and way == part // 2):
                start(doc_copy(way, hop + 1, part))

    def sys_take(hop):
        for way in range(2):
            sys_copy(way, hop).wait_recv()

    def sys_pass(hop):
        for way in range(2):
            start(sys_copy(way, hop + 1))

    for way in range(2):
        start(doc_copy(way, 1, 0))
    for k in (1, 3, 2):
        start(sys_y_copy(k))

    rows = make_plan(homes[...], docs_of[...], convs[...], y, z)
    plan_v[...] = jnp.concatenate(rows + [jnp.zeros((8 - len(rows), 128), jnp.int32)], axis=0)
    to_scalars = pltpu.make_async_copy(plan_v, plan, in_sem.at[5])
    to_scalars.start()

    loads[0].wait()
    to_scalars.wait()

    def tile_rows(a, b):
        parts = []
        for rows in (a, b):
            parts += [rows[:, h * DEPTH : (h + 1) * DEPTH] for h in range(HEADS)]
        return jnp.concatenate(parts, axis=0)

    def fill_own(s, carry):
        qin[s] = tile_rows(q_ref[plan[SLOT_A, s]], q_ref[plan[SLOT_B, s]])
        return carry

    def fill_group(g, carry):
        gq[g] = tile_rows(q_ref[plan[GRP_A, g]], q_ref[plan[GRP_B, g]])
        return carry

    for stage, (first, count) in enumerate(STAGES):

        def fill_out(i, carry, first=first, count=count):
            s = (1 + i // count) * NZ + first + i % count
            qs[s] = tile_rows(q_ref[plan[SLOT_A, s]], q_ref[plan[SLOT_B, s]])
            return carry

        lax.fori_loop(0, (NY - 1) * count, fill_out, 0)
        for k in (2, 1, 3):
            start(q_copy(k, stage))
    loads[1].wait()
    for k in range(1, NY):
        sys_y_copy(k).wait_recv()
    for way in range(2):
        start(sys_copy(way, 1))
    for part in range(1, PARTS):
        for way in range(2):
            start(doc_copy(way, 1, part))
    lax.fori_loop(0, NZ, fill_own, 0)
    lax.fori_loop(0, GROUPS, fill_group, 0)

    def attend(n, parts, done):
        def score(u, buf, part, top):
            first, size, score_of, _ = part
            s = score_of(u)
            buf[first : first + size] = s
            high = jnp.max(s.reshape(size // 8, 8, ROWS), axis=0)
            return high if top is None else jnp.maximum(top, high)

        def weigh(u, buf, part, top, state):
            first, size, _, mix_of = part
            e = jnp.exp2(buf[first : first + size] * SCALE2 - top)
            total = jnp.sum(e.reshape(size // 8, 8, ROWS), axis=0)
            o = mix_of(u, e.astype(BF16))
            return (o, total) if state is None else (state[0] + o, state[1] + total)

        def both(u_next, buf_next, u, buf, top):
            high = state = None
            for part in parts:
                high = score(u_next, buf_next, part, high)
                state = weigh(u, buf, part, top, state)
            done(u, state[0], jnp.sum(state[1], axis=0, keepdims=True), top)
            return jnp.max(high, axis=0, keepdims=True) * SCALE2

        def pair(i, top):
            top = both(2 * i + 1, s_b, 2 * i, s_a, top)
            return both(lax.rem(2 * i + 2, n), s_a, 2 * i + 1, s_b, top)

        high = None
        for part in parts:
            high = score(0, s_a, part, high)
        lax.fori_loop(0, n // 2, pair, jnp.max(high, axis=0, keepdims=True) * SCALE2)

    def doc_stage(stage):
        first, count = STAGES[stage]
        rel = PLACE_REL[first]
        for k in (1, 3, 2):
            q_copy(NY - k, stage).wait_recv()
        for j in range(count):
            vt[j] = docs[PLACE_REL[first + j], :, DEPTH:].T

        def place_of(u):
            return source_of(u // count) * NZ + first + u % count

        def rel_of(u):
            return rel + (u % count) * (NZ - 2 * rel)

        def part(at):
            keys = pl.ds(at, HALF)
            return (
                at, HALF,
                lambda u: scores(docs[rel_of(u), keys, :DEPTH], qin[place_of(u)]),
                lambda u, e: mix_t(vt[u % count, :, at : at + HALF], e),
            )

        def done(u, acc, total, top):
            ret_o[place_of(u)] = (acc * (1.0 / total)).astype(BF16)
            ret_l[place_of(u)] = top + jnp.log(total) * LOG2E
            send_back(u, stage)

        attend(NY * count, [part(0), part(HALF)], done)
        keep_own(stage)

    def source_of(i):
        return lax.rem(i + 1, NY)

    def send_back(u, stage):
        count = STAGES[stage][1]
        k = source_of(u // count)

        @pl.when((u % count == count - 1) & (k > 0))
        def _():
            o_copy(k, stage).start()
            e_copy(k, stage).start()

    def keep_own(stage):
        first, count = STAGES[stage]
        for k in range(1, NY):
            sent.append(o_copy(k, stage))
            sent.append(e_copy(k, stage))
        for j in range(first, first + count):
            d_o[j] = ret_o[j]
            d_l[j] = ret_l[j]

    def last_stage():
        stage = len(STAGES) - 1
        first, rel = STAGES[stage][0], PLACE_REL[STAGES[stage][0]]
        for k in (1, 3, 2):
            q_copy(NY - k, stage).wait_recv()

        def part(at):
            keys = pl.ds(at, PIECE)
            return (
                at, PIECE,
                lambda u: scores(docs[rel, keys, :DEPTH], qin[source_of(u) * NZ + first]),
                lambda u, e: mix_t(vt[0, :, at : at + PIECE], e),
            )

        def hold(u, acc, total, top):
            p_m[u] = top
            p_t[u] = total
            p_acc[u] = acc

        def done(u, acc, total, top):
            high = jnp.maximum(p_m[u], top)
            w_old = jnp.exp2(p_m[u] - high)
            w_new = jnp.exp2(top - high)
            total = p_t[u] * w_old + total * w_new
            place = source_of(u) * NZ + first
            ret_o[place] = ((p_acc[u] * w_old + acc * w_new) * (1.0 / total)).astype(BF16)
            ret_l[place] = high + jnp.log(total) * LOG2E
            send_back(u, stage)

        for pieces, finish in (((0, 2), hold), ((1, 3), done)):
            for piece in pieces:
                at = piece * PIECE
                doc_hop(4, piece)
                vt[0, :, at : at + PIECE] = docs[rel, at : at + PIECE, DEPTH:].T
            attend(NY, [part(piece * PIECE) for piece in pieces], finish)
        keep_own(stage)

    loads[3].wait()
    loads[4].wait()
    key_at = lax.broadcasted_iota(jnp.int32, (2 * SUF, ROWS), 0)
    row_at = lax.broadcasted_iota(jnp.int32, (2 * SUF, ROWS), 1)
    readable = (row_at // (SUF * HEADS) == key_at // SUF) & (key_at % SUF <= row_at % SUF)

    def own_tokens(g, lanes):
        return jnp.concatenate(
            [suf_ref[plan[GRP_A, g], :, lanes], suf_ref[plan[GRP_B, g], :, lanes]], axis=0
        )

    conv_parts = [
        (
            0, CONV,
            lambda g: scores(conv_ref[g, :, :DEPTH], gq[g]),
            lambda g, e: mix(conv_ref[g, :, DEPTH:], e),
        ),
        (
            CONV, 2 * SUF,
            lambda g: jnp.where(readable, scores(own_tokens(g, slice(0, DEPTH)), gq[g]), -1e30),
            lambda g, e: mix(own_tokens(g, slice(DEPTH, 2 * DEPTH)), e),
        ),
    ]

    def conv_done(g, acc, total, top):
        l_m[g] = top
        l_t[g] = total
        l_acc[g] = acc

    def sys_part(at, size):
        keys = pl.ds(at, size)
        return (
            at, size,
            lambda g: scores(sysb[keys, :DEPTH], gq[g]),
            lambda g, e: mix_t(sysvt[:, at : at + size], e),
        )

    def turn_sys(first, last):
        for place in range(first, last):
            at = place * SYS_Y
            sysvt[:, at : at + SYS_Y] = sysb[at : at + SYS_Y, DEPTH:].T

    def sys_done(g, acc, total, top):
        high = jnp.maximum(l_m[g], top)
        w_old = jnp.exp2(l_m[g] - high)
        w_new = jnp.exp2(top - high)
        l_m[g] = high
        l_t[g] = l_t[g] * w_old + total * w_new
        l_acc[g] = l_acc[g] * w_old + acc * w_new

    attend(GROUPS, conv_parts, conv_done)
    sys_take(1)
    sys_pass(1)
    doc_hop(1, 0)
    loads[2].wait()
    doc_stage(0)
    doc_hop(1, 1)
    doc_hop(1, 2)
    doc_hop(1, 3)
    doc_stage(1)
    sys_take(2)
    doc_hop(2, 0)
    turn_sys(0, 5)
    attend(GROUPS, [sys_part(0, 384), sys_part(384, SYS_FIRST - 384)], sys_done)
    doc_hop(2, 1)
    doc_hop(2, 2)
    doc_hop(2, 3)
    sys_pass(2)
    doc_stage(2)
    for part in range(PARTS):
        doc_hop(3, part)
    sys_take(3)
    sys_pass(3)
    doc_stage(3)
    last_stage()
    sys_take(4)
    turn_sys(5, 8)
    attend(GROUPS, [sys_part(SYS_FIRST, NZ * SYS_Y - SYS_FIRST)], sys_done)
    for stage in range(len(STAGES)):
        for k in range(1, NY):
            o_copy(k, stage).wait_recv()
            e_copy(k, stage).wait_recv()

    token = lax.broadcasted_iota(jnp.int32, (SUF, HEADS * DEPTH), 0)


    def join(r):
        at = plan[REQ_AT, r]
        g, second = at // 2, at % 2 == 1
        slot = plan[GRP_SLOT, g]

        def half(rows):
            return jnp.where(second, rows[:, ROWS // 2 :], rows[:, : ROWS // 2])

        lse, local, total = half(d_l[slot]), half(l_m[g]), half(l_t[g])
        top = jnp.maximum(lse, local)
        w_doc = jnp.exp2(lse - top)
        w_loc = jnp.exp2(local - top)
        upper = w_doc * half(d_o[slot]).astype(F32) + w_loc * half(l_acc[g])
        out = (upper / (w_doc + w_loc * total)).T.astype(BF16)
        rows = [out[h * SUF : (h + 1) * SUF] for h in range(HEADS)]
        value = jnp.concatenate(rows, axis=1)
        return jnp.where(token < lens[r], value, jnp.zeros_like(value))

    share = REQ // NT
    lanes = pl.ds(pl.multiple_of(tp * HEADS * DEPTH, 128), HEADS * DEPTH)

    def x_copy(k):
        return remote(
            outst.at[pl.ds(t_peer(k) * share, share)], out_hbm.at[:, :, lanes],
            x_ss.at[k - 1], x_rs.at[k - 1], (kv, t_peer(k)),
        )

    own = pltpu.make_async_copy(
        outst.at[pl.ds(tp * share, share)], out_hbm.at[:, :, lanes], in_sem.at[0]
    )
    for k in (4, 3, 5, 2, 6, 1, 7, 0):
        for i in range(share):
            r = t_peer(k) * share + i
            outst[r] = join(r)
        if k:
            start(x_copy(k))
        else:
            own.start()
    for copy in sent:
        copy.wait_send()
    own.wait()
    for k in range(1, NT):
        x_copy(k).wait_recv()


def on_device(queries, suffix_kv, suffix_len, sys_kv, doc_kv, doc_home, doc_of, conv_kv, conv_of):
    smem = pl.BlockSpec(memory_space=pltpu.SMEM)
    vmem = pl.BlockSpec(memory_space=pltpu.VMEM)
    hbm = pl.BlockSpec(memory_space=pl.ANY)
    dma = pltpu.SemaphoreType.DMA
    stages = len(STAGES)
    return pl.pallas_call(
        main_kernel,
        out_shape=pltpu.VMEM((REQ // NT, SUF, NT * HEADS * DEPTH), BF16),
        in_specs=[vmem] * 3 + [smem] + [hbm] * 5,
        out_specs=pl.BlockSpec(memory_space=pltpu.VMEM),
        scratch_shapes=[
            pltpu.VMEM((REQ, SUF, HEADS * DEPTH), BF16),
            pltpu.VMEM((REQ, SUF, 2 * DEPTH), BF16),
            pltpu.VMEM((GROUPS, CONV, 2 * DEPTH), BF16),
            pltpu.VMEM((NZ, DOC, 2 * DEPTH), BF16),
            pltpu.VMEM((NZ * SYS_Y, 2 * DEPTH), BF16),
            pltpu.VMEM((NY * NZ, ROWS, DEPTH), BF16),
            pltpu.VMEM((NY * NZ, ROWS, DEPTH), BF16),
            pltpu.VMEM((GROUPS, ROWS, DEPTH), BF16),
            pltpu.VMEM((2, DEPTH, DOC), BF16),
            pltpu.VMEM((DEPTH, NZ * SYS_Y), BF16),
            pltpu.VMEM((NY * NZ, DEPTH, ROWS), BF16),
            pltpu.VMEM((NY * NZ, 1, ROWS), F32),
            pltpu.VMEM((NY * NZ, DEPTH, ROWS), BF16),
            pltpu.VMEM((NY * NZ, 1, ROWS), F32),
            pltpu.VMEM((GROUPS, DEPTH, ROWS), F32),
            pltpu.VMEM((GROUPS, 1, ROWS), F32),
            pltpu.VMEM((GROUPS, 1, ROWS), F32),
            pltpu.VMEM((REQ, SUF, HEADS * DEPTH), BF16),
            pltpu.VMEM((DOC, ROWS), F32),
            pltpu.VMEM((DOC, ROWS), F32),
            pltpu.VMEM((NY, DEPTH, ROWS), F32),
            pltpu.VMEM((NY, 1, ROWS), F32),
            pltpu.VMEM((NY, 1, ROWS), F32),
            pltpu.VMEM((8, 128), jnp.int32),
            pltpu.SMEM((8, 128), jnp.int32),
            dma((6,)),
            dma((2, 4, PARTS)), dma((2, 4, PARTS)),
            dma((2, 4)), dma((2, 4)),
            dma((3,)), dma((3,)),
            dma((3, stages)), dma((3, stages)),
            dma((3, stages)), dma((3, stages)),
            dma((3, stages)), dma((3, stages)),
            dma((7,)), dma((7,)),
        ],
        compiler_params=pltpu.CompilerParams(
            collective_id=0, has_side_effects=True, vmem_limit_bytes=56 << 20
        ),
        name="cascade",
    )(
        doc_home.reshape(1, REQ),
        doc_of.reshape(1, REQ),
        conv_of.reshape(1, REQ),
        suffix_len,
        queries,
        suffix_kv.reshape(REQ, SUF, 2 * DEPTH),
        sys_kv.reshape(32, 2 * DEPTH),
        doc_kv.reshape(1, DOC, 2 * DEPTH),
        conv_kv.reshape(GROUPS, CONV, 2 * DEPTH),
    )


def solution(mesh):
    placed = (
        P("kv", None, "tp"),
        P("kv", None, "tp", None),
        P("kv"),
        P("kv", "tp", None),
        P("kv", None, "tp", None),
        P(),
        P("kv"),
        P("kv", None, "tp", None),
        P("kv"),
    )
    return jax.shard_map(
        on_device,
        mesh=mesh,
        in_specs=placed,
        out_specs=P(("kv", "tp"), None, None),
        check_vma=False,
    )
```
